768 devices in a mesh: gx: 8 (over y_lo, core), gy: 96 (over z, y_hi, x).
Axes of the slice: x: 4, y: 8 (y_hi: 2, y_lo: 4; y = y_hi * 4 + y_lo), z: 12, core: 2. Of those that a mesh axis runs over, the one named last changes fastest.
Arguments:
- electric_field: float32 [2, 3, 128, 1536, 128], P(None, None, 'gx', 'gy'), may hold values from -6 to 6
- magnetic_field: float32 [2, 3, 128, 1536, 128], P(None, None, 'gx', 'gy'), may hold values from -6 to 6
- material: int32 [128, 1536, 128], P('gx', 'gy'), may hold values from 0 to 7
- absorber_mask: int32 [128, 1536, 128], P('gx', 'gy'), may hold values 0 or 1
- permittivity: float32 [8], replicated, may hold values from 1 to 12
- conductivity: float32 [8], replicated, may hold values from 0 to 0.6
- bloch_phase: float32 [2], replicated, may hold values from -3.140625 to 3.140625
Outputs:
- electric_next: float32 [2, 3, 128, 1536, 128], P(None, None, 'gx', 'gy')
- magnetic_next: float32 [2, 3, 128, 1536, 128], P(None, None, 'gx', 'gy')
The draws below stay inside these ranges and needn't reach their ends.
Inputs may be any that keep to these rules, and one draw needn't show every extreme that they name: Every entry of `material` is an index from 0 to 7 into `permittivity` and `conductivity`.
All inputs are finite; a program needn't handle non-finite values. No bound on the sum of `absorber_mask` on one device may be relied on, other than what follows from the above.
Results may differ from the reference program's by a relative error of at most 0.00002.
Values sent between devices are 32-bit elements; how exact they have to be, the bound alone decides.
No kernel may reach another device: no remote copies, remote signals or barrier semaphores. Data moves between devices by JAX's collectives and lax.ppermute only.
A program may use at most 32 MiB of HBM per device.

```python
import math
import jax
import jax.numpy as jnp

NZ = 128
STEPS = 4
ABSORB = 10
MATS = 8
NX = 128
NY = 1536


def plant(drawn, stream_key, low, top_value):
    spot = [jax.random.randint(jax.random.fold_in(stream_key, axis), (), 0, length) for axis, length in enumerate(drawn.shape)]
    main_axis = drawn.shape.index(max(drawn.shape))
    neighbour = spot[:main_axis] + [(spot[main_axis] + 1) % drawn.shape[main_axis]] + spot[main_axis + 1:]
    return drawn.at[tuple(spot)].set(low).at[tuple(neighbour)].set(top_value)


def level_of(key, shape, cuts, smallest, high):
    def one(dim, shards_of):
        heights = jax.random.uniform(jax.random.fold_in(jax.random.fold_in(key, 6), dim), (shards_of,), jnp.float32, smallest / len(cuts), high / len(cuts))
        return jnp.repeat(jnp.exp(heights), shape[dim] // shards_of).reshape((-1,) + (1,) * (len(shape) - dim - 1))

    level = one(*cuts[0])
    for cut in cuts[1:]:
        level = level * one(*cut)
    return level


def normal_values(own_key, dims, scale, limit, split=(), held_as=jnp.bfloat16):
    result = jax.random.normal(own_key, dims, jnp.float32) * scale
    if len(split) > 0:
        result = level_of(own_key, dims, split, -0.22, 0.18) * result
    return jnp.clip(result, min=-limit, max=limit).astype(held_as)


def setup_inputs(seed: int = 0) -> dict:
    streams_of = jax.random.split(jax.random.key(seed), 8)
    return {
        "electric_field": normal_values(streams_of[0], (2, 3, NX, NY, NZ), 1.0, 6.0, ((2, 8), (3, 96)), jnp.float32),
        "magnetic_field": normal_values(streams_of[1], (2, 3, NX, NY, NZ), 1.0, 6.0, ((2, 8), (3, 96)), jnp.float32),
        "material": plant(jax.random.randint(streams_of[2], (NX, NY, NZ), 0, MATS), jax.random.fold_in(streams_of[2], 1), 0, MATS - 1).astype(jnp.int32),
        "absorber_mask": plant((jax.random.randint(streams_of[3], (NX, NY, NZ), 0, 4) < 3).astype(jnp.int32), jax.random.fold_in(streams_of[3], 1), 0, 1),
        "permittivity": jnp.clip(jnp.exp(jax.random.uniform(streams_of[4], (MATS,), jnp.float32, math.log(1.0), math.log(12.0))), 1.0, 12.0),
        "conductivity": jnp.clip(jax.random.uniform(streams_of[5], (MATS,), jnp.float32, 0.0, 0.6), 0.0, 0.6),
        "bloch_phase": jnp.clip(jax.random.uniform(streams_of[6], (2,), jnp.float32, -3.140625, 3.140625), -3.140625, 3.140625),
    }


TIME_STEP = 0.55
ABSORB_PEAK = 1.5


def rotate(complex_pair, turning):
    cosine_part = jnp.cos(turning)
    sine_part = jnp.sin(turning)
    return jnp.stack([complex_pair[0] * cosine_part - complex_pair[1] * sine_part,
                      complex_pair[0] * sine_part + complex_pair[1] * cosine_part])


def ahead_depth(values):
    return jnp.concatenate([values[..., 1:], jnp.zeros_like(values[..., :1])], -1)


def behind_depth(values):
    return jnp.concatenate([jnp.zeros_like(values[..., :1]), values[..., :-1]], -1)


def step_magnetic(electric, magnetic, decay, push, east_side, north_side):
    first_field, second_field, third_field = electric[:, 0], electric[:, 1], electric[:, 2]
    curl_first = (north_side[:, 1] - third_field) - (ahead_depth(second_field) - second_field)
    curl_second = (ahead_depth(first_field) - first_field) - (east_side[:, 1] - third_field)
    curl_third = (east_side[:, 0] - second_field) - (north_side[:, 0] - first_field)
    curl_all = jnp.stack([curl_first, curl_second, curl_third], 1)
    return decay * magnetic - push * curl_all


def step_electric(electric, magnetic, scale, drive, west_side, south_side):
    first_field, second_field, third_field = magnetic[:, 0], magnetic[:, 1], magnetic[:, 2]
    curl_first = (third_field - south_side[:, 1]) - (second_field - behind_depth(second_field))
    curl_second = (first_field - behind_depth(first_field)) - (third_field - west_side[:, 1])
    curl_third = (second_field - west_side[:, 0]) - (first_field - south_side[:, 0])
    curl_all = jnp.stack([curl_first, curl_second, curl_third], 1)
    return scale * electric + drive * curl_all


def coefficients(permittivity_cells, conductivity_cells, mask_cells):
    positions = jnp.arange(NZ).astype(jnp.float32)
    reach_depth = jnp.maximum(jnp.maximum(ABSORB - positions, positions - (NZ - 1 - ABSORB)), 0.0) / ABSORB
    profile = reach_depth * reach_depth * reach_depth
    magnetic_loss = mask_cells.astype(jnp.float32) * (ABSORB_PEAK * profile)
    electric_loss = conductivity_cells + magnetic_loss
    half_loss = electric_loss * (TIME_STEP / 2.0) / permittivity_cells
    scale = (1.0 - half_loss) / (1.0 + half_loss)
    drive = TIME_STEP / (permittivity_cells * (1.0 + half_loss))
    half_magnetic = magnetic_loss * (TIME_STEP / 2.0)
    decay = (1.0 - half_magnetic) / (1.0 + half_magnetic)
    push = TIME_STEP / (1.0 + half_magnetic)
    return scale, drive, decay, push


def reference(electric_field, magnetic_field, material, absorber_mask, permittivity, conductivity, bloch_phase):
    scale, drive, decay, push = coefficients(permittivity[material], conductivity[material], absorber_mask)
    phase_first = bloch_phase[0]
    phase_second = bloch_phase[1]
    electric = electric_field
    magnetic = magnetic_field
    for repeat in range(STEPS):
        lateral = electric[:, 1:3]
        east_side = jnp.concatenate([lateral[:, :, 1:], rotate(lateral[:, :, :1], phase_first)], 2)
        sideways = electric[:, ::2]
        north_side = jnp.concatenate([sideways[:, :, :, 1:], rotate(sideways[:, :, :, :1], phase_second)], 3)
        magnetic = step_magnetic(electric, magnetic, decay, push, east_side, north_side)
        lateral = magnetic[:, 1:3]
        west_side = jnp.concatenate([rotate(lateral[:, :, -1:], -phase_first), lateral[:, :, :-1]], 2)
        sideways = magnetic[:, ::2]
        south_side = jnp.concatenate([rotate(sideways[:, :, :, -1:], -phase_second), sideways[:, :, :, :-1]], 3)
        electric = step_electric(electric, magnetic, scale, drive, west_side, south_side)
    return electric, magnetic
```

```python
import jax
import jax.numpy as jnp
from jax import lax
from jax.experimental import pallas as pl
from jax.experimental.pallas import tpu as pltpu
from jax.sharding import PartitionSpec as P

ABSORB = 10
TIME_STEP = 0.55
ABSORB_PEAK = 1.5

OX, OY = 4, 8
XW, YW = 24, 32
LANES = 128
F32 = jnp.float32

TO_NEXT = (
    ("E", (0, 1, 2), (-3, -2, -1, 16, 17, 18, 19), 15),
    ("H", (0, 1, 2), (-3, -2, -1, 16, 17, 18), 15),
    ("H", (0, 1, 2), (-2, -1, 15, 16, 17, 18), 14),
    ("E", (0, 1, 2), (-1, 0, 15, 16, 17, 18), 14),
    ("H", (0, 2), (0, 14, 15, 16, 17), 13),
)
TO_PREV = (
    ("E", (0, 1, 2), (-4, -3, -2, -1, 16, 17, 18), 0),
    ("H", (0, 1, 2), (-4, -3, -2, -1, 15, 16, 17), 0),
    ("E", (0, 2), (-3, -2, -1, 0, 15, 16), 1),
    ("H", (0, 1, 2), (-3, -2, -1, 0, 14, 15), 1),
)
CELLS_NEXT = tuple((x, 15) for x in (-3, -2, -1, 16, 17, 18)) + tuple((x, 14) for x in (-1, 16, 17))
CELLS_PREV = tuple((x, 0) for x in (-3, -2, -1, 16, 17)) + tuple((x, 1) for x in (-2, -1))

X_TO_NEXT = (
    ("E", (0, 1, 2), (13,), 15),
    ("H", (0,), (13,), 15),
    ("E", (0, 1, 2), (12, 13), 0),
    ("H", (0, 1, 2), (12,), 0),
    ("H", (0,), (13,), 0),
    ("E", (0, 2), (13,), 1),
    ("H", (0,), (13,), 1),
    ("E", (0, 1, 2), (12,), 15),
    ("H", (1, 2), (12,), 15),
    ("E", (0, 1, 2), (13,), 14),
    ("H", (0,), (13,), 14),
)
X_TO_PREV = (
    ("E", (0, 1, 2), (2, 3), 15),
    ("H", (0, 1, 2), (2,), 15),
    ("H", (0, 1, 2), (2,), 14),
    ("E", (0, 1, 2), (2,), 14),
    ("E", (0, 1, 2), (2,), 0),
    ("H", (0, 1, 2), (2,), 0),
)
X_CELLS_NEXT = ((13, 15), (13, 0), (12, 15), (13, 14))
X_CELLS_PREV = ((2, 15), (2, 0))


def entries(face):
    return [(name, c, x, row) for name, comps, columns, row in face for c in comps for x in columns]


LIST_NEXT, LIST_PREV = entries(TO_NEXT), entries(TO_PREV)
HALF = max(len(LIST_NEXT), len(LIST_PREV))
CORNER_ROWS = -(-(2 * HALF + 2 * max(len(CELLS_NEXT), len(CELLS_PREV))) // 8) * 8

X_LIST_NEXT, X_LIST_PREV = entries(X_TO_NEXT), entries(X_TO_PREV)
X_HALF = max(len(X_LIST_NEXT), len(X_LIST_PREV))
X_SLABS = 32 + -(-(2 * X_HALF + 2 * len(X_CELLS_NEXT)) // 16)


def ghost_row(row):
    return row - 16 if row > 8 else row + 16


def lanes():
    return lax.broadcasted_iota(jnp.int32, (8, LANES), 1)


def ahead(v):
    return jnp.where(lanes() < LANES - 1, pltpu.roll(v, LANES - 1, 1), 0.0)


def behind(v):
    return jnp.where(lanes() > 0, pltpu.roll(v, 1, 1), 0.0)


def row_mask(start, low, high):
    y = lax.broadcasted_iota(jnp.int32, (8, LANES), 0) + (start - OY)
    return (y >= low) & (y < high)


def half_step(field, other, keep, gain, xlow, xhigh, windows, sign):
    along_z = ahead if sign == 1 else behind
    for X in range(xlow + OX, xhigh + OX):
        for start, low, high in windows:
            s, n = pl.ds(start, 8), pl.ds(start + sign, 8)
            whole = low <= start - OY and high >= start - OY + 8
            d, q = keep[X, s, :], gain[X, s, :]
            for p in range(2):
                fx, fy, fz = (other[p, c, X, s, :] for c in range(3))
                y_x, y_z = other[p, 0, X, n, :], other[p, 2, X, n, :]
                x_y, x_z = other[p, 1, X + sign, s, :], other[p, 2, X + sign, s, :]
                curl = (
                    (y_z - fz) - (along_z(fy) - fy),
                    (along_z(fx) - fx) - (x_z - fz),
                    (x_y - fy) - (y_x - fx),
                )
                for c in range(3):
                    old = field[p, c, X, s, :]
                    new = d * old - q * curl[c]
                    field[p, c, X, s, :] = new if whole else jnp.where(row_mask(start, low, high), new, old)


def half_h(E, H, decay, push, xlow, xhigh, windows):
    half_step(H, E, decay, push, xlow, xhigh, windows, 1)


def half_e(E, H, scale, drive, xlow, xhigh, windows):
    half_step(E, H, scale, drive, xlow, xhigh, windows, -1)


def own(low, high):
    return ((8, low, high), (16, low, high))


SIGMA, X_TURN, Y_TURN = 8, 16, 18


def coefficients(table, material, mask):
    eps = jnp.broadcast_to(table[0:1, :], material.shape)
    sigma = jnp.broadcast_to(table[SIGMA : SIGMA + 1, :], material.shape)
    for m in range(1, 8):
        chosen = material == float(m)
        eps = jnp.where(chosen, table[m : m + 1, :], eps)
        sigma = jnp.where(chosen, table[SIGMA + m : SIGMA + m + 1, :], sigma)
    k = lax.broadcasted_iota(jnp.int32, (1, LANES), 1).astype(F32)
    reach = jnp.maximum(jnp.maximum(ABSORB - k, k - (LANES - 1 - ABSORB)), 0.0) / ABSORB
    magnetic_loss = mask * (ABSORB_PEAK * (reach * reach * reach))
    half = (sigma + magnetic_loss) * (TIME_STEP / 2.0) / eps
    below = 1.0 / (1.0 + half)
    half_m = magnetic_loss * (TIME_STEP / 2.0)
    below_m = 1.0 / (1.0 + half_m)
    return (1.0 - half) * below, (TIME_STEP / eps) * below, (1.0 - half_m) * below_m, TIME_STEP * below_m


def set_coefficients(table, state, X, s, material, mask):
    for ref, value in zip(state, coefficients(table, material, mask)):
        ref[X, s, :] = value


def edge_turn(axis, angle):
    index = lax.axis_index(axis)
    return jnp.where(index == 0, -angle, jnp.where(index == lax.axis_size(axis) - 1, angle, 0.0))


def is_odd(axis):
    return lax.rem(lax.axis_index(axis), 2) == 1


def either(odd, make, a, b):
    pl.when(odd)(lambda: make(b, a))
    pl.when(jnp.logical_not(odd))(lambda: make(a, b))


def turned(table, row, re, im):
    cosine, sine = table[row : row + 1, :], table[row + 1 : row + 2, :]
    return re * cosine - im * sine, re * sine + im * cosine


def pack_y(buf, E, H, mat, mask, rows, extra):
    for x in range(16):
        X = x + OX
        for p in range(2):
            for c in range(3):
                at = 4 * (3 * p + c)
                buf[x, at : at + 2, :] = E[p, c, X, rows : rows + 2, :]
                buf[x, at + 2 : at + 4, :] = H[p, c, X, rows : rows + 2, :]
        if extra is not None:
            for p in range(2):
                for i, c in enumerate((0, 2)):
                    at = 24 + 2 * p + i
                    buf[x, at : at + 1, :] = H[p, c, X, extra : extra + 1, :]
        buf[x, 28:30, :] = mat[X, rows : rows + 2, :]
        buf[x, 30:32, :] = mask[X, rows : rows + 2, :]


def pack_x(buf, E, H, mat, mask, first, extra, items, cells):
    columns, rows = pl.ds(first + OX, 2), pl.ds(OY, 16)
    for p in range(2):
        for c in range(3):
            at = 2 * (3 * p + c)
            buf[at : at + 2] = E[p, c, columns, rows, :]
            buf[12 + at : 14 + at] = H[p, c, columns, rows, :]
    if extra is not None:
        for p in range(2):
            for i, c in enumerate((1, 2)):
                buf[24 + 2 * p + i] = H[p, c, extra + OX, rows, :]
    buf[28:30] = mat[columns, rows, :]
    buf[30:32] = mask[columns, rows, :]

    def put(row, value):
        buf[32 + row // 16, row % 16 : row % 16 + 1, :] = value

    pack_rows(put, E, H, mat, mask, items, cells, X_HALF)


def pack_rows(put, E, H, mat, mask, items, cells, half):
    for i, (name, c, x, row) in enumerate(items):
        field = E if name == "E" else H
        for p in range(2):
            put(p * half + i, field[p, c, x + OX, row + OY : row + OY + 1, :])
    for i, (x, row) in enumerate(cells):
        put(2 * half + 2 * i, mat[x + OX, row + OY : row + OY + 1, :])
        put(2 * half + 2 * i + 1, mask[x + OX, row + OY : row + OY + 1, :])


def unpack_rows(get, E, H, mat, mask, items, cells, half, turn, place):
    for i, (name, c, x, row) in enumerate(items):
        field = E if name == "E" else H
        X, R = place(x, row)
        re, im = turn(get(i), get(half + i))
        field[0, c, X, R : R + 1, :] = re
        field[1, c, X, R : R + 1, :] = im
    for i, (x, row) in enumerate(cells):
        X, R = place(x, row)
        mat[X, R : R + 1, :] = get(2 * half + 2 * i)
        mask[X, R : R + 1, :] = get(2 * half + 2 * i + 1)


def first_kernel(
    e_in, h_in, mat_in, mask_in, eps_in, sigma_in, phase_in,
    E, H, scale, drive, decay, push, mat, mask, table, xa, xb, ya, yb,
    raw_mat, raw_mask, eps, sigma, phase, sems,
):
    state = (scale, drive, decay, push)
    inside = (slice(None), slice(None), pl.ds(OX, 16), pl.ds(OY, 16), slice(None))
    pairs = [
        (eps_in, eps),
        (sigma_in, sigma),
        (phase_in, phase),
        (mat_in, raw_mat),
        (mask_in, raw_mask),
        (e_in, E.at[inside]),
        (h_in, H.at[inside]),
    ]
    copies = [pltpu.make_async_copy(a, b, sems.at[i]) for i, (a, b) in enumerate(pairs)]
    for copy in copies:
        copy.start()
    for copy in copies[:3]:
        copy.wait()
    for m in range(8):
        table[m : m + 1, :] = jnp.full((1, LANES), eps[m], F32)
        table[SIGMA + m : SIGMA + m + 1, :] = jnp.full((1, LANES), sigma[m], F32)
    for axis, row, i in (("gx", X_TURN, 0), ("gy", Y_TURN, 1)):
        angle = jnp.full((1, LANES), edge_turn(axis, phase[i]), F32)
        table[row : row + 1, :] = jnp.cos(angle)
        table[row + 1 : row + 2, :] = jnp.sin(angle)
    copies[3].wait()
    copies[4].wait()
    for x in range(16):
        for start in (0, 8):
            s, t = pl.ds(start, 8), pl.ds(start + OY, 8)
            m, k = raw_mat[x, s, :].astype(F32), raw_mask[x, s, :].astype(F32)
            mat[x + OX, t, :] = m
            mask[x + OX, t, :] = k
            set_coefficients(table, state, x + OX, t, m, k)
    copies[5].wait()
    copies[6].wait()

    half_h(E, H, decay, push, 0, 15, own(0, 15))
    half_e(E, H, scale, drive, 1, 15, own(1, 15))
    half_h(E, H, decay, push, 1, 14, own(1, 14))

    def x_faces(to_next, to_prev):
        pack_x(to_next, E, H, mat, mask, 14, 13, X_LIST_NEXT, X_CELLS_NEXT)
        pack_x(to_prev, E, H, mat, mask, 0, None, X_LIST_PREV, X_CELLS_PREV)

    def y_faces(to_next, to_prev):
        pack_y(to_next, E, H, mat, mask, OY + 14, OY + 13)
        pack_y(to_prev, E, H, mat, mask, OY, None)

    either(is_odd("gx"), x_faces, xa, xb)
    either(is_odd("gy"), y_faces, ya, yb)


def second_kernel(
    xb, xa, table, e_io, h_io, s_io, d_io, c_io, p_io, m_io, k_io,
    E, H, scale, drive, decay, push, mat, mask, ya, yb,
):
    state = (scale, drive, decay, push)
    rows = pl.ds(OY, 16)

    def place(buf, first, extra, items, cells, shift, edge):
        def turn(re, im):
            return turned(table, X_TURN, re, im) if edge else (re, im)

        for field, base in ((E, 0), (H, 12)):
            for c in range(3):
                at = base + 2 * c
                for j in range(2):
                    re, im = turn(buf[at + j], buf[at + 6 + j])
                    field[0, c, first + OX + j, rows, :] = re
                    field[1, c, first + OX + j, rows, :] = im
        if extra is not None:
            for i, c in enumerate((1, 2)):
                re, im = turn(buf[24 + i], buf[26 + i])
                H[0, c, extra + OX, rows, :] = re
                H[1, c, extra + OX, rows, :] = im
        for j in range(2):
            X = first + OX + j
            for start in (0, 8):
                s, t = pl.ds(start, 8), pl.ds(start + OY, 8)
                m, k = buf[28 + j, s, :], buf[30 + j, s, :]
                mat[X, t, :] = m
                mask[X, t, :] = k
                set_coefficients(table, state, X, t, m, k)

        def get(row):
            return buf[32 + row // 16, row % 16 : row % 16 + 1, :]

        unpack_rows(
            get, E, H, mat, mask, items, cells, X_HALF, turn, lambda x, row: (x + shift + OX, row + OY)
        )

    def ghosts(above, below, odd):
        place(below, -2, -3, X_LIST_NEXT, X_CELLS_NEXT, -16, not odd)
        place(above, 16, None, X_LIST_PREV, X_CELLS_PREV, 16, odd)

    gx_odd = is_odd("gx")
    pl.when(gx_odd)(lambda: ghosts(xb, xa, True))
    pl.when(jnp.logical_not(gx_odd))(lambda: ghosts(xa, xb, False))

    for X in (0, 1, 22):
        for start in (8, 16):
            s = pl.ds(start, 8)
            set_coefficients(table, state, X, s, mat[X, s, :], mask[X, s, :])

    half_h(E, H, decay, push, -1, 0, own(0, 15))
    half_h(E, H, decay, push, 15, 16, own(0, 15))
    half_e(E, H, scale, drive, -1, 1, own(1, 15))
    half_e(E, H, scale, drive, 15, 17, own(1, 15))
    half_h(E, H, decay, push, -2, 1, own(1, 14))
    half_h(E, H, decay, push, 14, 17, own(1, 14))

    def pack(to_next, to_prev):
        for buf, items, cells in ((to_next, LIST_NEXT, CELLS_NEXT), (to_prev, LIST_PREV, CELLS_PREV)):

            def put(row, value, buf=buf):
                buf[row : row + 1, :] = value

            pack_rows(put, E, H, mat, mask, items, cells, HALF)

    either(is_odd("gy"), pack, ya, yb)


def third_kernel(
    e_io, h_io, s_io, d_io, c_io, p_io,
    E, H, scale, drive, decay, push,
):
    half_e(E, H, scale, drive, -2, 18, own(2, 14))
    half_h(E, H, decay, push, -2, 17, own(2, 13))
    half_e(E, H, scale, drive, -1, 17, own(3, 13))
    half_h(E, H, decay, push, -1, 16, own(3, 12))
    half_e(E, H, scale, drive, 0, 16, own(4, 12))


def last_kernel(
    yb, ya, zb, za, table, e_io, h_io, s_io, d_io, c_io, p_io,
    e_out, h_out, E, H, scale, drive, decay, push,
    mat, mask, sems,
):
    state = (scale, drive, decay, push)

    def unpack_y(buf, rows, extra, edge):
        def turn(re, im):
            return turned(table, Y_TURN, re, im) if edge else (re, im)

        for x in range(16):
            X = x + OX
            for c in range(3):
                for f, field in enumerate((E, H)):
                    re, im = (buf[x, 4 * (3 * p + c) + 2 * f : 4 * (3 * p + c) + 2 * f + 2, :] for p in range(2))
                    re, im = turn(re, im)
                    field[0, c, X, rows : rows + 2, :] = re
                    field[1, c, X, rows : rows + 2, :] = im
            if extra is not None:
                for i, c in enumerate((0, 2)):
                    re, im = turn(buf[x, 24 + i : 25 + i, :], buf[x, 26 + i : 27 + i, :])
                    H[0, c, X, extra : extra + 1, :] = re
                    H[1, c, X, extra : extra + 1, :] = im
            mat[X, rows : rows + 2, :] = buf[x, 28:30, :]
            mask[X, rows : rows + 2, :] = buf[x, 30:32, :]

    def ghosts(above, below, above_far, below_far, odd):
        unpack_y(below, OY - 2, OY - 3, not odd)
        unpack_y(above, OY + 16, None, odd)
        for buf, items, cells, edge in (
            (below_far, LIST_NEXT, CELLS_NEXT, not odd),
            (above_far, LIST_PREV, CELLS_PREV, odd),
        ):

            def turn(re, im, edge=edge):
                return turned(table, Y_TURN, re, im) if edge else (re, im)

            unpack_rows(
                lambda row, buf=buf: buf[row : row + 1, :],
                E, H, mat, mask, items, cells, HALF, turn,
                lambda x, row: (x + OX, ghost_row(row) + OY),
            )

    gy_odd = is_odd("gy")
    pl.when(gy_odd)(lambda: ghosts(yb, ya, zb, za, True))
    pl.when(jnp.logical_not(gy_odd))(lambda: ghosts(ya, yb, za, zb, False))

    for X in range(1, XW - 1):
        for start in (0, 24):
            s = pl.ds(start, 8)
            set_coefficients(table, state, X, s, mat[X, s, :], mask[X, s, :])

    def sides(low, low_end, high, high_end):
        return ((4, low, low_end), (20, high, high_end))

    half_h(E, H, decay, push, -4, 19, sides(-1, 0, 15, 16))
    half_e(E, H, scale, drive, -3, 19, sides(-1, 1, 15, 17))
    half_h(E, H, decay, push, -3, 18, sides(-2, 1, 14, 17))
    half_e(E, H, scale, drive, -2, 18, sides(-2, 2, 14, 18))
    half_h(E, H, decay, push, -2, 17, sides(-2, 2, 13, 17))
    half_e(E, H, scale, drive, -1, 17, sides(-1, 3, 13, 17))
    half_h(E, H, decay, push, -1, 16, sides(-1, 3, 12, 16))
    inside = (slice(None), slice(None), pl.ds(OX, 16), pl.ds(OY, 16), slice(None))
    copy_h = pltpu.make_async_copy(H.at[inside], h_out, sems.at[0])
    copy_h.start()
    half_e(E, H, scale, drive, 0, 16, sides(0, 4, 12, 16))
    copy_e = pltpu.make_async_copy(E.at[inside], e_out, sems.at[1])
    copy_e.start()
    copy_h.wait()
    copy_e.wait()


VMEM = pl.BlockSpec(memory_space=pltpu.VMEM)
HBM = pl.BlockSpec(memory_space=pltpu.HBM)
FIELD = jax.ShapeDtypeStruct((2, 3, XW, YW, LANES), F32)
CELL = jax.ShapeDtypeStruct((XW, YW, LANES), F32)
TABLE = jax.ShapeDtypeStruct((24, LANES), F32)
X_FACE = jax.ShapeDtypeStruct((X_SLABS, 16, LANES), F32)
Y_FACE = jax.ShapeDtypeStruct((16, 32, LANES), F32)
FAR_FACE = jax.ShapeDtypeStruct((CORNER_ROWS, LANES), F32)
PARAMS = pltpu.CompilerParams(vmem_limit_bytes=32 * 1024 * 1024)


def swapped(value, axis, odd):
    count = lax.axis_size(axis)
    pairs = []
    for low in range(odd, count, 2):
        high = (low + 1) % count
        pairs += [(low, high), (high, low)]
    return lax.ppermute(value, axis, pairs)


def per_device(electric, magnetic, material, absorber_mask, permittivity, conductivity, bloch_phase):
    out = pl.pallas_call(
        first_kernel,
        out_shape=(FIELD, FIELD) + (CELL,) * 6 + (TABLE, X_FACE, X_FACE, Y_FACE, Y_FACE),
        in_specs=[HBM] * 7,
        out_specs=(VMEM,) * 13,
        scratch_shapes=[
            pltpu.VMEM((16, 16, LANES), jnp.int32),
            pltpu.VMEM((16, 16, LANES), jnp.int32),
            pltpu.SMEM((8,), F32),
            pltpu.SMEM((8,), F32),
            pltpu.SMEM((2,), F32),
            pltpu.SemaphoreType.DMA((7,)),
        ],
        compiler_params=PARAMS,
        name="first",
    )(*(pltpu.with_memory_space_constraint(v, pltpu.HBM) for v in (electric, magnetic, material, absorber_mask, permittivity, conductivity, bloch_phase)))
    state, table, (xa, xb, ya, yb) = out[:8], out[8], out[9:]
    xb = swapped(xb, "gx", 1)
    yb = swapped(yb, "gy", 1)
    xa = swapped(xa, "gx", 0)
    ya = swapped(ya, "gy", 0)
    out = pl.pallas_call(
        second_kernel,
        out_shape=(FIELD, FIELD) + (CELL,) * 6 + (FAR_FACE, FAR_FACE),
        in_specs=[VMEM] * 11,
        out_specs=(VMEM,) * 10,
        input_output_aliases={3 + i: i for i in range(8)},
        compiler_params=PARAMS,
        name="second",
    )(xb, xa, table, *state)
    state, (za, zb) = out[:6], out[8:]
    zb = swapped(zb, "gy", 1)
    za = swapped(za, "gy", 0)
    state = pl.pallas_call(
        third_kernel,
        out_shape=(FIELD, FIELD) + (CELL,) * 4,
        in_specs=[VMEM] * 6,
        out_specs=(VMEM,) * 6,
        input_output_aliases={i: i for i in range(6)},
        compiler_params=PARAMS,
        name="third",
    )(*state)
    out = pl.pallas_call(
        last_kernel,
        out_shape=(
            jax.ShapeDtypeStruct(electric.shape, F32),
            jax.ShapeDtypeStruct(magnetic.shape, F32),
            FIELD,
            FIELD,
        )
        + (CELL,) * 4,
        in_specs=[VMEM] * 11,
        out_specs=(HBM, HBM) + (VMEM,) * 6,
        input_output_aliases={5 + i: 2 + i for i in range(6)},
        scratch_shapes=[
            pltpu.VMEM(CELL.shape, F32),
            pltpu.VMEM(CELL.shape, F32),
            pltpu.SemaphoreType.DMA((2,)),
        ],
        compiler_params=PARAMS,
        name="last",
    )(yb, ya, zb, za, table, *state)
    return out[0], out[1]


def solution(mesh):
    field = P(None, None, "gx", "gy", None)
    cell = P("gx", "gy", None)
    return jax.shard_map(
        per_device,
        mesh=mesh,
        in_specs=(field, field, cell, cell, P(), P(), P()),
        out_specs=(field, field),
        check_vma=False,
    )
```

```python
import jax
import jax.numpy as jnp
from jax import lax
from jax.experimental import pallas as pl
from jax.experimental.pallas import tpu as pltpu
from jax.sharding import PartitionSpec as P

ABSORB = 10
TIME_STEP = 0.55
ABSORB_PEAK = 1.5

OX, OY = 4, 8
XW, YW = 24, 32
LANES = 128
F32 = jnp.float32

TO_NEXT = (
    ("E", (0, 1, 2), (-3, -2, -1, 16, 17, 18, 19), 15),
    ("H", (0, 1, 2), (-3, -2, -1, 16, 17, 18), 15),
    ("H", (0, 1, 2), (-2, -1, 16, 17, 18), 14),
    ("E", (0, 1, 2), (-1, 16, 17, 18), 14),
    ("H", (0, 2), (16, 17), 13),
)
TO_PREV = (
    ("E", (0, 1, 2), (-4, -3, -2, -1, 16, 17, 18), 0),
    ("H", (0, 1, 2), (-4, -3, -2, -1, 16, 17), 0),
    ("E", (0, 2), (-3, -2, -1, 16), 1),
    ("H", (0, 1, 2), (-3, -2, -1), 1),
)
CELLS_NEXT = tuple((x, 15) for x in (-3, -2, -1, 16, 17, 18)) + tuple((x, 14) for x in (-1, 16, 17))
CELLS_PREV = tuple((x, 0) for x in (-3, -2, -1, 16, 17)) + tuple((x, 1) for x in (-2, -1))

X_TO_NEXT = (
    ("E", (0, 1, 2), (13,), 15),
    ("H", (0,), (13,), 15),
    ("E", (0, 1, 2), (12, 13), 0),
    ("H", (0, 1, 2), (12,), 0),
    ("H", (0,), (13,), 0),
    ("E", (0, 2), (13,), 1),
    ("H", (0,), (13,), 1),
    ("E", (0, 1, 2), (12,), 15),
    ("H", (1, 2), (12,), 15),
    ("E", (0, 1, 2), (13,), 14),
    ("H", (0,), (13,), 14),
)
X_TO_PREV = (
    ("E", (0, 1, 2), (2, 3), 15),
    ("H", (0, 1, 2), (2,), 15),
    ("H", (0, 1, 2), (2,), 14),
    ("E", (0, 1, 2), (2,), 14),
    ("E", (0, 1, 2), (2,), 0),
    ("H", (0, 1, 2), (2,), 0),
)
X_CELLS_NEXT = ((13, 15), (13, 0), (12, 15), (13, 14))
X_CELLS_PREV = ((2, 15), (2, 0))


def entries(face):
    return [(name, c, x, row) for name, comps, columns, row in face for c in comps for x in columns]


LIST_NEXT, LIST_PREV = entries(TO_NEXT), entries(TO_PREV)
HALF = max(len(LIST_NEXT), len(LIST_PREV))
FAR = 16 * 32
Y_ROWS = FAR + -(-(2 * HALF + 2 * max(len(CELLS_NEXT), len(CELLS_PREV))) // 8) * 8

X_LIST_NEXT, X_LIST_PREV = entries(X_TO_NEXT), entries(X_TO_PREV)
X_HALF = max(len(X_LIST_NEXT), len(X_LIST_PREV))
X_SLABS = 32 + -(-(2 * X_HALF + 2 * len(X_CELLS_NEXT)) // 16)


def ghost_row(row):
    return row - 16 if row > 8 else row + 16


def lanes():
    return lax.broadcasted_iota(jnp.int32, (8, LANES), 1)


def ahead(v):
    return jnp.where(lanes() < LANES - 1, pltpu.roll(v, LANES - 1, 1), 0.0)


def behind(v):
    return jnp.where(lanes() > 0, pltpu.roll(v, 1, 1), 0.0)


def row_mask(start, low, high):
    y = lax.broadcasted_iota(jnp.int32, (8, LANES), 0) + (start - OY)
    return (y >= low) & (y < high)


def half_step(field, other, keep, gain, xlow, xhigh, windows, sign):
    along_z = ahead if sign == 1 else behind
    for X in range(xlow + OX, xhigh + OX):
        for start, low, high in windows:
            s, n = pl.ds(start, 8), pl.ds(start + sign, 8)
            whole = low <= start - OY and high >= start - OY + 8
            d, q = keep[X, s, :], gain[X, s, :]
            for p in range(2):
                fx, fy, fz = (other[p, c, X, s, :] for c in range(3))
                y_x, y_z = other[p, 0, X, n, :], other[p, 2, X, n, :]
                x_y, x_z = other[p, 1, X + sign, s, :], other[p, 2, X + sign, s, :]
                curl = (
                    (y_z - fz) - (along_z(fy) - fy),
                    (along_z(fx) - fx) - (x_z - fz),
                    (x_y - fy) - (y_x - fx),
                )
                for c in range(3):
                    old = field[p, c, X, s, :]
                    new = d * old - q * curl[c]
                    field[p, c, X, s, :] = new if whole else jnp.where(row_mask(start, low, high), new, old)


def half_h(E, H, decay, push, xlow, xhigh, windows):
    half_step(H, E, decay, push, xlow, xhigh, windows, 1)


def half_e(E, H, scale, drive, xlow, xhigh, windows):
    half_step(E, H, scale, drive, xlow, xhigh, windows, -1)


def own(low, high):
    return ((8, low, high), (16, low, high))


SIGMA, X_TURN, Y_TURN = 8, 16, 18


def coefficients(table, material, mask):
    eps = jnp.broadcast_to(table[0:1, :], material.shape)
    sigma = jnp.broadcast_to(table[SIGMA : SIGMA + 1, :], material.shape)
    for m in range(1, 8):
        chosen = material == float(m)
        eps = jnp.where(chosen, table[m : m + 1, :], eps)
        sigma = jnp.where(chosen, table[SIGMA + m : SIGMA + m + 1, :], sigma)
    k = lax.broadcasted_iota(jnp.int32, (1, LANES), 1).astype(F32)
    reach = jnp.maximum(jnp.maximum(ABSORB - k, k - (LANES - 1 - ABSORB)), 0.0) / ABSORB
    magnetic_loss = mask * (ABSORB_PEAK * (reach * reach * reach))
    half = (sigma + magnetic_loss) * (TIME_STEP / 2.0) / eps
    below = 1.0 / (1.0 + half)
    half_m = magnetic_loss * (TIME_STEP / 2.0)
    below_m = 1.0 / (1.0 + half_m)
    return (1.0 - half) * below, (TIME_STEP / eps) * below, (1.0 - half_m) * below_m, TIME_STEP * below_m


def set_coefficients(table, state, X, s, material, mask):
    for ref, value in zip(state, coefficients(table, material, mask)):
        ref[X, s, :] = value


def edge_turn(axis, angle):
    index = lax.axis_index(axis)
    return jnp.where(index == 0, -angle, jnp.where(index == lax.axis_size(axis) - 1, angle, 0.0))


def is_odd(axis):
    return lax.rem(lax.axis_index(axis), 2) == 1


def either(odd, make, a, b):
    pl.when(odd)(lambda: make(b, a))
    pl.when(jnp.logical_not(odd))(lambda: make(a, b))


def turned(table, row, re, im):
    cosine, sine = table[row : row + 1, :], table[row + 1 : row + 2, :]
    return re * cosine - im * sine, re * sine + im * cosine


def pack_y(buf, E, H, mat, mask, rows, extra, items, cells):
    for x in range(16):
        X, base = x + OX, 32 * x
        for p in range(2):
            for c in range(3):
                at = base + 4 * (3 * p + c)
                buf[at : at + 2, :] = E[p, c, X, rows : rows + 2, :]
                buf[at + 2 : at + 4, :] = H[p, c, X, rows : rows + 2, :]
        if extra is not None:
            for p in range(2):
                for i, c in enumerate((0, 2)):
                    at = base + 24 + 2 * p + i
                    buf[at : at + 1, :] = H[p, c, X, extra : extra + 1, :]
        buf[base + 28 : base + 30, :] = mat[X, rows : rows + 2, :]
        buf[base + 30 : base + 32, :] = mask[X, rows : rows + 2, :]

    def put(row, value):
        buf[FAR + row : FAR + row + 1, :] = value

    pack_rows(put, E, H, mat, mask, items, cells, HALF)


def unpack_y(buf, table, E, H, state, mat, mask, below, edge):
    rows, extra, tile = (OY - 2, OY - 3, 0) if below else (OY + 16, None, 24)

    def turn(re, im):
        return turned(table, Y_TURN, re, im) if edge else (re, im)

    for x in range(16):
        X, base = x + OX, 32 * x
        for c in range(3):
            for f, field in enumerate((E, H)):
                at = [base + 4 * (3 * p + c) + 2 * f for p in range(2)]
                re, im = turn(buf[at[0] : at[0] + 2, :], buf[at[1] : at[1] + 2, :])
                field[0, c, X, rows : rows + 2, :] = re
                field[1, c, X, rows : rows + 2, :] = im
        if extra is not None:
            for i, c in enumerate((0, 2)):
                at = base + 24 + i
                re, im = turn(buf[at : at + 1, :], buf[at + 2 : at + 3, :])
                H[0, c, X, extra : extra + 1, :] = re
                H[1, c, X, extra : extra + 1, :] = im
        mat[X, rows - tile : rows - tile + 2, :] = buf[base + 28 : base + 30, :]
        mask[X, rows - tile : rows - tile + 2, :] = buf[base + 30 : base + 32, :]

    def place(x, row):
        return x + OX, ghost_row(row) + OY

    unpack_rows(
        lambda row: buf[FAR + row : FAR + row + 1, :],
        E, H, mat, mask,
        LIST_NEXT if below else LIST_PREV,
        CELLS_NEXT if below else CELLS_PREV,
        HALF, turn, place, tile,
    )
    for X in range(1, XW - 1):
        set_coefficients(table, state, X, pl.ds(tile, 8), mat[X, :, :], mask[X, :, :])


def pack_x(buf, E, H, mat, mask, first, extra, items, cells):
    columns, rows = pl.ds(first + OX, 2), pl.ds(OY, 16)
    for p in range(2):
        for c in range(3):
            at = 2 * (3 * p + c)
            buf[at : at + 2] = E[p, c, columns, rows, :]
            buf[12 + at : 14 + at] = H[p, c, columns, rows, :]
    if extra is not None:
        for p in range(2):
            for i, c in enumerate((1, 2)):
                buf[24 + 2 * p + i] = H[p, c, extra + OX, rows, :]
    buf[28:30] = mat[columns, rows, :]
    buf[30:32] = mask[columns, rows, :]

    def put(row, value):
        buf[32 + row // 16, row % 16 : row % 16 + 1, :] = value

    pack_rows(put, E, H, mat, mask, items, cells, X_HALF)


def pack_rows(put, E, H, mat, mask, items, cells, half):
    for i, (name, c, x, row) in enumerate(items):
        field = E if name == "E" else H
        for p in range(2):
            put(p * half + i, field[p, c, x + OX, row + OY : row + OY + 1, :])
    for i, (x, row) in enumerate(cells):
        put(2 * half + 2 * i, mat[x + OX, row + OY : row + OY + 1, :])
        put(2 * half + 2 * i + 1, mask[x + OX, row + OY : row + OY + 1, :])


def unpack_rows(get, E, H, mat, mask, items, cells, half, turn, place, tile=0):
    for i, (name, c, x, row) in enumerate(items):
        field = E if name == "E" else H
        X, R = place(x, row)
        re, im = turn(get(i), get(half + i))
        field[0, c, X, R : R + 1, :] = re
        field[1, c, X, R : R + 1, :] = im
    for i, (x, row) in enumerate(cells):
        X, R = place(x, row)
        mat[X, R - tile : R - tile + 1, :] = get(2 * half + 2 * i)
        mask[X, R - tile : R - tile + 1, :] = get(2 * half + 2 * i + 1)


def first_kernel(
    e_in, h_in, mat_in, mask_in, eps_in, sigma_in, phase_in,
    E, H, scale, drive, decay, push, mat, mask, table, xa, xb,
    raw_mat, raw_mask, eps, sigma, phase, sems,
):
    state = (scale, drive, decay, push)
    inside = (slice(None), slice(None), pl.ds(OX, 16), pl.ds(OY, 16), slice(None))
    pairs = [
        (eps_in, eps),
        (sigma_in, sigma),
        (phase_in, phase),
        (mat_in, raw_mat),
        (mask_in, raw_mask),
        (e_in, E.at[inside]),
        (h_in, H.at[inside]),
    ]
    copies = [pltpu.make_async_copy(a, b, sems.at[i]) for i, (a, b) in enumerate(pairs)]
    for copy in copies:
        copy.start()
    for copy in copies[:3]:
        copy.wait()
    for m in range(8):
        table[m : m + 1, :] = jnp.full((1, LANES), eps[m], F32)
        table[SIGMA + m : SIGMA + m + 1, :] = jnp.full((1, LANES), sigma[m], F32)
    for axis, row, i in (("gx", X_TURN, 0), ("gy", Y_TURN, 1)):
        angle = jnp.full((1, LANES), edge_turn(axis, phase[i]), F32)
        table[row : row + 1, :] = jnp.cos(angle)
        table[row + 1 : row + 2, :] = jnp.sin(angle)
    copies[3].wait()
    copies[4].wait()
    for x in range(16):
        for start in (0, 8):
            s, t = pl.ds(start, 8), pl.ds(start + OY, 8)
            m, k = raw_mat[x, s, :].astype(F32), raw_mask[x, s, :].astype(F32)
            mat[x + OX, t, :] = m
            mask[x + OX, t, :] = k
            set_coefficients(table, state, x + OX, t, m, k)
    copies[5].wait()
    copies[6].wait()

    half_h(E, H, decay, push, 0, 15, own(0, 15))
    half_e(E, H, scale, drive, 1, 15, own(1, 15))
    half_h(E, H, decay, push, 1, 14, own(1, 14))

    def x_faces(to_next, to_prev):
        pack_x(to_next, E, H, mat, mask, 14, 13, X_LIST_NEXT, X_CELLS_NEXT)
        pack_x(to_prev, E, H, mat, mask, 0, None, X_LIST_PREV, X_CELLS_PREV)

    either(is_odd("gx"), x_faces, xa, xb)


def second_kernel(
    xb, xa, table, e_io, h_io, s_io, d_io, c_io, p_io, m_io, k_io,
    E, H, scale, drive, decay, push, mat, mask, ya, yb,
):
    state = (scale, drive, decay, push)
    rows = pl.ds(OY, 16)

    def place(buf, first, extra, items, cells, shift, edge):
        def turn(re, im):
            return turned(table, X_TURN, re, im) if edge else (re, im)

        for field, base in ((E, 0), (H, 12)):
            for c in range(3):
                at = base + 2 * c
                for j in range(2):
                    re, im = turn(buf[at + j], buf[at + 6 + j])
                    field[0, c, first + OX + j, rows, :] = re
                    field[1, c, first + OX + j, rows, :] = im
        if extra is not None:
            for i, c in enumerate((1, 2)):
                re, im = turn(buf[24 + i], buf[26 + i])
                H[0, c, extra + OX, rows, :] = re
                H[1, c, extra + OX, rows, :] = im
        for j in range(2):
            X = first + OX + j
            for start in (0, 8):
                s, t = pl.ds(start, 8), pl.ds(start + OY, 8)
                m, k = buf[28 + j, s, :], buf[30 + j, s, :]
                mat[X, t, :] = m
                mask[X, t, :] = k
                set_coefficients(table, state, X, t, m, k)

        def get(row):
            return buf[32 + row // 16, row % 16 : row % 16 + 1, :]

        unpack_rows(
            get, E, H, mat, mask, items, cells, X_HALF, turn, lambda x, row: (x + shift + OX, row + OY)
        )

    def ghosts(above, below, odd):
        place(below, -2, -3, X_LIST_NEXT, X_CELLS_NEXT, -16, not odd)
        place(above, 16, None, X_LIST_PREV, X_CELLS_PREV, 16, odd)

    gx_odd = is_odd("gx")
    pl.when(gx_odd)(lambda: ghosts(xb, xa, True))
    pl.when(jnp.logical_not(gx_odd))(lambda: ghosts(xa, xb, False))

    for X in (0, 1, 22):
        for start in (8, 16):
            s = pl.ds(start, 8)
            set_coefficients(table, state, X, s, mat[X, s, :], mask[X, s, :])

    half_h(E, H, decay, push, -1, 0, own(0, 15))
    half_h(E, H, decay, push, 15, 16, own(0, 15))
    half_e(E, H, scale, drive, -1, 1, own(1, 15))
    half_e(E, H, scale, drive, 15, 17, own(1, 15))
    half_h(E, H, decay, push, -2, 1, own(1, 14))
    half_h(E, H, decay, push, 14, 17, own(1, 14))

    def pack(to_next, to_prev):
        pack_y(to_next, E, H, mat, mask, OY + 14, OY + 13, LIST_NEXT, CELLS_NEXT)
        pack_y(to_prev, E, H, mat, mask, OY, None, LIST_PREV, CELLS_PREV)

    either(is_odd("gy"), pack, ya, yb)


def third_kernel(
    e_io, h_io, s_io, d_io, c_io, p_io,
    E, H, scale, drive, decay, push,
):
    half_e(E, H, scale, drive, -2, 18, own(2, 14))
    half_h(E, H, decay, push, -2, 17, own(2, 13))
    half_e(E, H, scale, drive, -1, 17, own(3, 13))
    half_h(E, H, decay, push, -1, 16, own(3, 12))
    half_e(E, H, scale, drive, 0, 16, own(4, 12))


def fourth_kernel(
    ya, table, e_io, h_io, s_io, d_io, c_io, p_io,
    E, H, scale, drive, decay, push,
    mat, mask,
):
    gy_odd = is_odd("gy")
    args = (ya, table, E, H, (scale, drive, decay, push), mat, mask)
    pl.when(gy_odd)(lambda: unpack_y(*args, True, False))
    pl.when(jnp.logical_not(gy_odd))(lambda: unpack_y(*args, False, False))


def last_kernel(
    yb, table, e_io, h_io, s_io, d_io, c_io, p_io,
    e_out, h_out, E, H, scale, drive, decay, push,
    mat, mask, sems,
):
    gy_odd = is_odd("gy")
    args = (yb, table, E, H, (scale, drive, decay, push), mat, mask)
    pl.when(gy_odd)(lambda: unpack_y(*args, False, True))
    pl.when(jnp.logical_not(gy_odd))(lambda: unpack_y(*args, True, True))

    def sides(low, low_end, high, high_end):
        return ((4, low, low_end), (20, high, high_end))

    half_h(E, H, decay, push, -4, 19, sides(-1, 0, 15, 16))
    half_e(E, H, scale, drive, -3, 19, sides(-1, 1, 15, 17))
    half_h(E, H, decay, push, -3, 18, sides(-2, 1, 14, 17))
    half_e(E, H, scale, drive, -2, 18, sides(-2, 2, 14, 18))
    half_h(E, H, decay, push, -2, 17, sides(-2, 2, 13, 17))
    half_e(E, H, scale, drive, -1, 17, sides(-1, 3, 13, 17))
    half_h(E, H, decay, push, -1, 16, sides(-1, 3, 12, 16))
    inside = (slice(None), slice(None), pl.ds(OX, 16), pl.ds(OY, 16), slice(None))
    copy_h = pltpu.make_async_copy(H.at[inside], h_out, sems.at[0])
    copy_h.start()
    half_e(E, H, scale, drive, 0, 16, sides(0, 4, 12, 16))
    copy_e = pltpu.make_async_copy(E.at[inside], e_out, sems.at[1])
    copy_e.start()
    copy_h.wait()
    copy_e.wait()


VMEM = pl.BlockSpec(memory_space=pltpu.VMEM)
HBM = pl.BlockSpec(memory_space=pltpu.HBM)
FIELD = jax.ShapeDtypeStruct((2, 3, XW, YW, LANES), F32)
CELL = jax.ShapeDtypeStruct((XW, YW, LANES), F32)
TABLE = jax.ShapeDtypeStruct((24, LANES), F32)
X_FACE = jax.ShapeDtypeStruct((X_SLABS, 16, LANES), F32)
Y_FACE = jax.ShapeDtypeStruct((Y_ROWS, LANES), F32)
PARAMS = pltpu.CompilerParams(vmem_limit_bytes=32 * 1024 * 1024)


def swapped(value, axis, odd):
    count = lax.axis_size(axis)
    pairs = []
    for low in range(odd, count, 2):
        high = (low + 1) % count
        pairs += [(low, high), (high, low)]
    return lax.ppermute(value, axis, pairs)


def per_device(electric, magnetic, material, absorber_mask, permittivity, conductivity, bloch_phase):
    out = pl.pallas_call(
        first_kernel,
        out_shape=(FIELD, FIELD) + (CELL,) * 6 + (TABLE, X_FACE, X_FACE),
        in_specs=[HBM] * 7,
        out_specs=(VMEM,) * 11,
        scratch_shapes=[
            pltpu.VMEM((16, 16, LANES), jnp.int32),
            pltpu.VMEM((16, 16, LANES), jnp.int32),
            pltpu.SMEM((8,), F32),
            pltpu.SMEM((8,), F32),
            pltpu.SMEM((2,), F32),
            pltpu.SemaphoreType.DMA((7,)),
        ],
        compiler_params=PARAMS,
        name="first",
    )(*(pltpu.with_memory_space_constraint(v, pltpu.HBM) for v in (electric, magnetic, material, absorber_mask, permittivity, conductivity, bloch_phase)))
    state, table, (xa, xb) = out[:8], out[8], out[9:]
    xb = swapped(xb, "gx", 1)
    xa = swapped(xa, "gx", 0)
    out = pl.pallas_call(
        second_kernel,
        out_shape=(FIELD, FIELD) + (CELL,) * 6 + (Y_FACE, Y_FACE),
        in_specs=[VMEM] * 11,
        out_specs=(VMEM,) * 10,
        input_output_aliases={3 + i: i for i in range(8)},
        compiler_params=PARAMS,
        name="second",
    )(xb, xa, table, *state)
    state, (ya, yb) = out[:6], out[8:]
    yb = swapped(yb, "gy", 1)
    ya = swapped(ya, "gy", 0)
    state = pl.pallas_call(
        third_kernel,
        out_shape=(FIELD, FIELD) + (CELL,) * 4,
        in_specs=[VMEM] * 6,
        out_specs=(VMEM,) * 6,
        input_output_aliases={i: i for i in range(6)},
        compiler_params=PARAMS,
        cost_estimate=pl.CostEstimate(flops=20000000000, bytes_accessed=0, transcendentals=0),
        name="third",
    )(*state)
    state = pl.pallas_call(
        fourth_kernel,
        out_shape=(FIELD, FIELD) + (CELL,) * 4,
        in_specs=[VMEM] * 8,
        out_specs=(VMEM,) * 6,
        input_output_aliases={2 + i: i for i in range(6)},
        scratch_shapes=[pltpu.VMEM((XW, 8, LANES), F32), pltpu.VMEM((XW, 8, LANES), F32)],
        compiler_params=PARAMS,
        name="fourth",
    )(ya, table, *state)
    out = pl.pallas_call(
        last_kernel,
        out_shape=(
            jax.ShapeDtypeStruct(electric.shape, F32),
            jax.ShapeDtypeStruct(magnetic.shape, F32),
            FIELD,
            FIELD,
        )
        + (CELL,) * 4,
        in_specs=[VMEM] * 8,
        out_specs=(HBM, HBM) + (VMEM,) * 6,
        input_output_aliases={2 + i: 2 + i for i in range(6)},
        scratch_shapes=[
            pltpu.VMEM((XW, 8, LANES), F32),
            pltpu.VMEM((XW, 8, LANES), F32),
            pltpu.SemaphoreType.DMA((2,)),
        ],
        compiler_params=PARAMS,
        name="last",
    )(yb, table, *state)
    return out[0], out[1]


def solution(mesh):
    field = P(None, None, "gx", "gy", None)
    cell = P("gx", "gy", None)
    return jax.shard_map(
        per_device,
        mesh=mesh,
        in_specs=(field, field, cell, cell, P(), P(), P()),
        out_specs=(field, field),
        check_vma=False,
    )
```

```python
import jax
import jax.numpy as jnp
from jax import lax
from jax.experimental import pallas as pl
from jax.experimental.pallas import tpu as pltpu
from jax.sharding import PartitionSpec as P

ABSORB = 10
TIME_STEP = 0.55
ABSORB_PEAK = 1.5

OX, OY = 4, 8
XW, YW = 24, 32
LANES = 128
F32 = jnp.float32

TO_NEXT = (
    ("E", (0, 1, 2), (-3, -2, -1, 16, 17, 18, 19), 15),
    ("H", (0, 1, 2), (-3, -2, -1, 16, 17, 18), 15),
    ("H", (0, 1, 2), (-2, -1, 16, 17, 18), 14),
    ("E", (0, 1, 2), (-1, 16, 17, 18), 14),
    ("H", (0, 2), (16, 17), 13),
)
TO_PREV = (
    ("E", (0, 1, 2), (-4, -3, -2, -1, 16, 17, 18), 0),
    ("H", (0, 1, 2), (-4, -3, -2, -1, 16, 17), 0),
    ("E", (0, 2), (-3, -2, -1, 16), 1),
    ("H", (0, 1, 2), (-3, -2, -1), 1),
)
CELLS_NEXT = tuple((x, 15) for x in (-3, -2, -1, 16, 17, 18)) + tuple((x, 14) for x in (-1, 16, 17))
CELLS_PREV = tuple((x, 0) for x in (-3, -2, -1, 16, 17)) + tuple((x, 1) for x in (-2, -1))

X_TO_NEXT = (
    ("E", (0, 1, 2), (13,), 15),
    ("H", (0,), (13,), 15),
    ("E", (0, 1, 2), (12, 13), 0),
    ("H", (0, 1, 2), (12,), 0),
    ("H", (0,), (13,), 0),
    ("E", (0, 2), (13,), 1),
    ("H", (0,), (13,), 1),
    ("E", (0, 1, 2), (12,), 15),
    ("H", (1, 2), (12,), 15),
    ("E", (0, 1, 2), (13,), 14),
    ("H", (0,), (13,), 14),
)
X_TO_PREV = (
    ("E", (0, 1, 2), (2, 3), 15),
    ("H", (0, 1, 2), (2,), 15),
    ("H", (0, 1, 2), (2,), 14),
    ("E", (0, 1, 2), (2,), 14),
    ("E", (0, 1, 2), (2,), 0),
    ("H", (0, 1, 2), (2,), 0),
)
X_CELLS_NEXT = ((13, 15), (13, 0), (12, 15), (13, 14))
X_CELLS_PREV = ((2, 15), (2, 0))


def entries(face):
    return [(name, c, x, row) for name, comps, columns, row in face for c in comps for x in columns]


LIST_NEXT, LIST_PREV = entries(TO_NEXT), entries(TO_PREV)
HALF = max(len(LIST_NEXT), len(LIST_PREV))
FAR = 16 * 32
Y_ROWS = FAR + -(-(2 * HALF + 2 * max(len(CELLS_NEXT), len(CELLS_PREV))) // 8) * 8

X_LIST_NEXT, X_LIST_PREV = entries(X_TO_NEXT), entries(X_TO_PREV)
X_HALF = max(len(X_LIST_NEXT), len(X_LIST_PREV))
X_SLABS = 32 + -(-(2 * X_HALF + 2 * len(X_CELLS_NEXT)) // 16)


def ghost_row(row):
    return row - 16 if row > 8 else row + 16


def lanes():
    return lax.broadcasted_iota(jnp.int32, (8, LANES), 1)


def ahead(v):
    return jnp.where(lanes() < LANES - 1, pltpu.roll(v, LANES - 1, 1), 0.0)


def behind(v):
    return jnp.where(lanes() > 0, pltpu.roll(v, 1, 1), 0.0)


def row_mask(start, low, high):
    y = lax.broadcasted_iota(jnp.int32, (8, LANES), 0) + (start - OY)
    return (y >= low) & (y < high)


def half_step(field, other, keep, gain, xlow, xhigh, windows, sign):
    along_z = ahead if sign == 1 else behind
    beside = {
        (X, start, p, c): along_z(other[p, c, X, pl.ds(start, 8), :])
        for X in range(xlow + OX, xhigh + OX)
        for start, _, _ in windows
        for p in range(2)
        for c in (1, 0)
    }
    for X in range(xlow + OX, xhigh + OX):
        for start, low, high in windows:
            s, n = pl.ds(start, 8), pl.ds(start + sign, 8)
            whole = low <= start - OY and high >= start - OY + 8
            d, q = keep[X, s, :], gain[X, s, :]
            for p in range(2):
                fx, fy, fz = (other[p, c, X, s, :] for c in range(3))
                y_x, y_z = other[p, 0, X, n, :], other[p, 2, X, n, :]
                x_y, x_z = other[p, 1, X + sign, s, :], other[p, 2, X + sign, s, :]
                curl = (
                    (y_z - fz) - (beside[X, start, p, 1] - fy),
                    (beside[X, start, p, 0] - fx) - (x_z - fz),
                    (x_y - fy) - (y_x - fx),
                )
                for c in range(3):
                    old = field[p, c, X, s, :]
                    new = d * old - q * curl[c]
                    field[p, c, X, s, :] = new if whole else jnp.where(row_mask(start, low, high), new, old)


def half_h(E, H, decay, push, xlow, xhigh, windows):
    half_step(H, E, decay, push, xlow, xhigh, windows, 1)


def half_e(E, H, scale, drive, xlow, xhigh, windows):
    half_step(E, H, scale, drive, xlow, xhigh, windows, -1)


def own(low, high):
    return ((8, low, high), (16, low, high))


SIGMA, X_TURN, Y_TURN = 8, 16, 18


def coefficients(table, material, mask):
    eps = jnp.broadcast_to(table[0:1, :], material.shape)
    sigma = jnp.broadcast_to(table[SIGMA : SIGMA + 1, :], material.shape)
    for m in range(1, 8):
        chosen = material == float(m)
        eps = jnp.where(chosen, table[m : m + 1, :], eps)
        sigma = jnp.where(chosen, table[SIGMA + m : SIGMA + m + 1, :], sigma)
    k = lax.broadcasted_iota(jnp.int32, (1, LANES), 1).astype(F32)
    reach = jnp.maximum(jnp.maximum(ABSORB - k, k - (LANES - 1 - ABSORB)), 0.0) / ABSORB
    magnetic_loss = mask * (ABSORB_PEAK * (reach * reach * reach))
    half = (sigma + magnetic_loss) * (TIME_STEP / 2.0) / eps
    below = 1.0 / (1.0 + half)
    half_m = magnetic_loss * (TIME_STEP / 2.0)
    below_m = 1.0 / (1.0 + half_m)
    return (1.0 - half) * below, (TIME_STEP / eps) * below, (1.0 - half_m) * below_m, TIME_STEP * below_m


def set_coefficients(table, state, X, s, material, mask):
    for ref, value in zip(state, coefficients(table, material, mask)):
        ref[X, s, :] = value


def edge_turn(axis, angle):
    index = lax.axis_index(axis)
    return jnp.where(index == 0, -angle, jnp.where(index == lax.axis_size(axis) - 1, angle, 0.0))


def is_odd(axis):
    return lax.rem(lax.axis_index(axis), 2) == 1


def either(odd, make, a, b):
    pl.when(odd)(lambda: make(b, a))
    pl.when(jnp.logical_not(odd))(lambda: make(a, b))


def turned(table, row, re, im):
    cosine, sine = table[row : row + 1, :], table[row + 1 : row + 2, :]
    return re * cosine - im * sine, re * sine + im * cosine


def pack_y(buf, E, H, mat, mask, rows, extra, items, cells):
    for x in range(16):
        X, base = x + OX, 32 * x
        for p in range(2):
            for c in range(3):
                at = base + 4 * (3 * p + c)
                buf[at : at + 2, :] = E[p, c, X, rows : rows + 2, :]
                buf[at + 2 : at + 4, :] = H[p, c, X, rows : rows + 2, :]
        if extra is not None:
            for p in range(2):
                for i, c in enumerate((0, 2)):
                    at = base + 24 + 2 * p + i
                    buf[at : at + 1, :] = H[p, c, X, extra : extra + 1, :]
        buf[base + 28 : base + 30, :] = mat[X, rows : rows + 2, :]
        buf[base + 30 : base + 32, :] = mask[X, rows : rows + 2, :]

    def put(row, value):
        buf[FAR + row : FAR + row + 1, :] = value

    pack_rows(put, E, H, mat, mask, items, cells, HALF)


def unpack_y(buf, table, E, H, state, mat, mask, below, edge):
    rows, extra, tile = (OY - 2, OY - 3, 0) if below else (OY + 16, None, 24)

    def turn(re, im):
        return turned(table, Y_TURN, re, im) if edge else (re, im)

    for x in range(16):
        X, base = x + OX, 32 * x
        for c in range(3):
            for f, field in enumerate((E, H)):
                at = [base + 4 * (3 * p + c) + 2 * f for p in range(2)]
                re, im = turn(buf[at[0] : at[0] + 2, :], buf[at[1] : at[1] + 2, :])
                field[0, c, X, rows : rows + 2, :] = re
                field[1, c, X, rows : rows + 2, :] = im
        if extra is not None:
            for i, c in enumerate((0, 2)):
                at = base + 24 + i
                re, im = turn(buf[at : at + 1, :], buf[at + 2 : at + 3, :])
                H[0, c, X, extra : extra + 1, :] = re
                H[1, c, X, extra : extra + 1, :] = im
        mat[X, rows - tile : rows - tile + 2, :] = buf[base + 28 : base + 30, :]
        mask[X, rows - tile : rows - tile + 2, :] = buf[base + 30 : base + 32, :]

    def place(x, row):
        return x + OX, ghost_row(row) + OY

    unpack_rows(
        lambda row: buf[FAR + row : FAR + row + 1, :],
        E, H, mat, mask,
        LIST_NEXT if below else LIST_PREV,
        CELLS_NEXT if below else CELLS_PREV,
        HALF, turn, place, tile,
    )
    for X in range(1, XW - 1):
        set_coefficients(table, state, X, pl.ds(tile, 8), mat[X, :, :], mask[X, :, :])


def pack_x(buf, E, H, mat, mask, first, extra, items, cells):
    columns, rows = pl.ds(first + OX, 2), pl.ds(OY, 16)
    for p in range(2):
        for c in range(3):
            at = 2 * (3 * p + c)
            buf[at : at + 2] = E[p, c, columns, rows, :]
            buf[12 + at : 14 + at] = H[p, c, columns, rows, :]
    if extra is not None:
        for p in range(2):
            for i, c in enumerate((1, 2)):
                buf[24 + 2 * p + i] = H[p, c, extra + OX, rows, :]
    buf[28:30] = mat[columns, rows, :]
    buf[30:32] = mask[columns, rows, :]

    def put(row, value):
        buf[32 + row // 16, row % 16 : row % 16 + 1, :] = value

    pack_rows(put, E, H, mat, mask, items, cells, X_HALF)


def pack_rows(put, E, H, mat, mask, items, cells, half):
    for i, (name, c, x, row) in enumerate(items):
        field = E if name == "E" else H
        for p in range(2):
            put(p * half + i, field[p, c, x + OX, row + OY : row + OY + 1, :])
    for i, (x, row) in enumerate(cells):
        put(2 * half + 2 * i, mat[x + OX, row + OY : row + OY + 1, :])
        put(2 * half + 2 * i + 1, mask[x + OX, row + OY : row + OY + 1, :])


def unpack_rows(get, E, H, mat, mask, items, cells, half, turn, place, tile=0):
    for i, (name, c, x, row) in enumerate(items):
        field = E if name == "E" else H
        X, R = place(x, row)
        re, im = turn(get(i), get(half + i))
        field[0, c, X, R : R + 1, :] = re
        field[1, c, X, R : R + 1, :] = im
    for i, (x, row) in enumerate(cells):
        X, R = place(x, row)
        mat[X, R - tile : R - tile + 1, :] = get(2 * half + 2 * i)
        mask[X, R - tile : R - tile + 1, :] = get(2 * half + 2 * i + 1)


def first_kernel(
    e_in, h_in, mat_in, mask_in, eps_in, sigma_in, phase_in,
    E, H, scale, drive, decay, push, mat, mask, table, xa, xb,
    raw_mat, raw_mask, eps, sigma, phase, sems,
):
    state = (scale, drive, decay, push)
    inside = (slice(None), slice(None), pl.ds(OX, 16), pl.ds(OY, 16), slice(None))
    pairs = [
        (eps_in, eps),
        (sigma_in, sigma),
        (phase_in, phase),
        (mat_in, raw_mat),
        (mask_in, raw_mask),
        (e_in, E.at[inside]),
        (h_in, H.at[inside]),
    ]
    copies = [pltpu.make_async_copy(a, b, sems.at[i]) for i, (a, b) in enumerate(pairs)]
    for copy in copies:
        copy.start()
    for copy in copies[:3]:
        copy.wait()
    for m in range(8):
        table[m : m + 1, :] = jnp.full((1, LANES), eps[m], F32)
        table[SIGMA + m : SIGMA + m + 1, :] = jnp.full((1, LANES), sigma[m], F32)
    for axis, row, i in (("gx", X_TURN, 0), ("gy", Y_TURN, 1)):
        angle = jnp.full((1, LANES), edge_turn(axis, phase[i]), F32)
        table[row : row + 1, :] = jnp.cos(angle)
        table[row + 1 : row + 2, :] = jnp.sin(angle)
    copies[3].wait()
    copies[4].wait()
    for x in range(16):
        for start in (0, 8):
            s, t = pl.ds(start, 8), pl.ds(start + OY, 8)
            m, k = raw_mat[x, s, :].astype(F32), raw_mask[x, s, :].astype(F32)
            mat[x + OX, t, :] = m
            mask[x + OX, t, :] = k
            set_coefficients(table, state, x + OX, t, m, k)
    copies[5].wait()
    copies[6].wait()

    half_h(E, H, decay, push, 0, 15, own(0, 15))
    half_e(E, H, scale, drive, 1, 15, own(1, 15))
    half_h(E, H, decay, push, 1, 14, own(1, 14))

    def x_faces(to_next, to_prev):
        pack_x(to_next, E, H, mat, mask, 14, 13, X_LIST_NEXT, X_CELLS_NEXT)
        pack_x(to_prev, E, H, mat, mask, 0, None, X_LIST_PREV, X_CELLS_PREV)

    either(is_odd("gx"), x_faces, xa, xb)


def second_kernel(
    xb, xa, table, e_io, h_io, s_io, d_io, c_io, p_io, m_io, k_io,
    E, H, scale, drive, decay, push, mat, mask, ya, yb,
):
    state = (scale, drive, decay, push)
    rows = pl.ds(OY, 16)

    def place(buf, first, extra, items, cells, shift, edge):
        def turn(re, im):
            return turned(table, X_TURN, re, im) if edge else (re, im)

        for field, base in ((E, 0), (H, 12)):
            for c in range(3):
                at = base + 2 * c
                for j in range(2):
                    re, im = turn(buf[at + j], buf[at + 6 + j])
                    field[0, c, first + OX + j, rows, :] = re
                    field[1, c, first + OX + j, rows, :] = im
        if extra is not None:
            for i, c in enumerate((1, 2)):
                re, im = turn(buf[24 + i], buf[26 + i])
                H[0, c, extra + OX, rows, :] = re
                H[1, c, extra + OX, rows, :] = im
        for j in range(2):
            X = first + OX + j
            for start in (0, 8):
                s, t = pl.ds(start, 8), pl.ds(start + OY, 8)
                m, k = buf[28 + j, s, :], buf[30 + j, s, :]
                mat[X, t, :] = m
                mask[X, t, :] = k
                set_coefficients(table, state, X, t, m, k)

        def get(row):
            return buf[32 + row // 16, row % 16 : row % 16 + 1, :]

        unpack_rows(
            get, E, H, mat, mask, items, cells, X_HALF, turn, lambda x, row: (x + shift + OX, row + OY)
        )

    def ghosts(above, below, odd):
        place(below, -2, -3, X_LIST_NEXT, X_CELLS_NEXT, -16, not odd)
        place(above, 16, None, X_LIST_PREV, X_CELLS_PREV, 16, odd)

    gx_odd = is_odd("gx")
    pl.when(gx_odd)(lambda: ghosts(xb, xa, True))
    pl.when(jnp.logical_not(gx_odd))(lambda: ghosts(xa, xb, False))

    for X in (0, 1, 22):
        for start in (8, 16):
            s = pl.ds(start, 8)
            set_coefficients(table, state, X, s, mat[X, s, :], mask[X, s, :])

    half_h(E, H, decay, push, -1, 0, own(0, 15))
    half_h(E, H, decay, push, 15, 16, own(0, 15))
    half_e(E, H, scale, drive, -1, 1, own(1, 15))
    half_e(E, H, scale, drive, 15, 17, own(1, 15))
    half_h(E, H, decay, push, -2, 1, own(1, 14))
    half_h(E, H, decay, push, 14, 17, own(1, 14))

    def pack(to_next, to_prev):
        pack_y(to_next, E, H, mat, mask, OY + 14, OY + 13, LIST_NEXT, CELLS_NEXT)
        pack_y(to_prev, E, H, mat, mask, OY, None, LIST_PREV, CELLS_PREV)

    either(is_odd("gy"), pack, ya, yb)


def third_kernel(
    e_io, h_io, s_io, d_io, c_io, p_io,
    E, H, scale, drive, decay, push,
):
    half_e(E, H, scale, drive, -2, 18, own(2, 14))
    half_h(E, H, decay, push, -2, 17, own(2, 13))
    half_e(E, H, scale, drive, -1, 17, own(3, 13))
    half_h(E, H, decay, push, -1, 16, own(3, 12))
    half_e(E, H, scale, drive, 0, 16, own(4, 12))


def fourth_kernel(
    ya, table, e_io, h_io, s_io, d_io, c_io, p_io,
    E, H, scale, drive, decay, push,
    mat, mask,
):
    gy_odd = is_odd("gy")
    args = (ya, table, E, H, (scale, drive, decay, push), mat, mask)
    pl.when(gy_odd)(lambda: unpack_y(*args, True, False))
    pl.when(jnp.logical_not(gy_odd))(lambda: unpack_y(*args, False, False))


def last_kernel(
    yb, table, e_io, h_io, s_io, d_io, c_io, p_io,
    e_out, h_out, E, H, scale, drive, decay, push,
    mat, mask, sems,
):
    gy_odd = is_odd("gy")
    args = (yb, table, E, H, (scale, drive, decay, push), mat, mask)
    pl.when(gy_odd)(lambda: unpack_y(*args, False, True))
    pl.when(jnp.logical_not(gy_odd))(lambda: unpack_y(*args, True, True))

    def sides(low, low_end, high, high_end):
        return ((4, low, low_end), (20, high, high_end))

    copies = []
    for part, (start, end) in enumerate(((None, 8), (8, 16))):

        def span(low, shift, high, start=start, end=end):
            return low if start is None else start + shift, high if end == 16 else end + shift

        half_h(E, H, decay, push, *span(-4, 3, 19), sides(-1, 0, 15, 16))
        half_e(E, H, scale, drive, *span(-3, 3, 19), sides(-1, 1, 15, 17))
        half_h(E, H, decay, push, *span(-3, 2, 18), sides(-2, 1, 14, 17))
        half_e(E, H, scale, drive, *span(-2, 2, 18), sides(-2, 2, 14, 18))
        half_h(E, H, decay, push, *span(-2, 1, 17), sides(-2, 2, 13, 17))
        half_e(E, H, scale, drive, *span(-1, 1, 17), sides(-1, 3, 13, 17))
        half_h(E, H, decay, push, *span(-1, 0, 16), sides(-1, 3, 12, 16))
        copies += copy_out(H, h_out, sems.at[2 * part], end - 8)
        half_e(E, H, scale, drive, *span(0, 0, 16), sides(0, 4, 12, 16))
        copies += copy_out(E, e_out, sems.at[2 * part + 1], end - 8)
    for copy in copies:
        copy.wait()


def copy_out(field, out, sem, first):
    copies = []
    for p in range(2):
        for c in range(3):
            copy = pltpu.make_async_copy(
                field.at[p, c, pl.ds(first + OX, 8), pl.ds(OY, 16)], out.at[p, c, pl.ds(first, 8)], sem.at[3 * p + c]
            )
            copy.start()
            copies.append(copy)
    return copies


VMEM = pl.BlockSpec(memory_space=pltpu.VMEM)
HBM = pl.BlockSpec(memory_space=pltpu.HBM)
FIELD = jax.ShapeDtypeStruct((2, 3, XW, YW, LANES), F32)
CELL = jax.ShapeDtypeStruct((XW, YW, LANES), F32)
TABLE = jax.ShapeDtypeStruct((24, LANES), F32)
X_FACE = jax.ShapeDtypeStruct((X_SLABS, 16, LANES), F32)
Y_FACE = jax.ShapeDtypeStruct((Y_ROWS, LANES), F32)
PARAMS = pltpu.CompilerParams(vmem_limit_bytes=32 * 1024 * 1024)


def swapped(value, axis, odd):
    count = lax.axis_size(axis)
    pairs = []
    for low in range(odd, count, 2):
        high = (low + 1) % count
        pairs += [(low, high), (high, low)]
    return lax.ppermute(value, axis, pairs)


def per_device(electric, magnetic, material, absorber_mask, permittivity, conductivity, bloch_phase):
    out = pl.pallas_call(
        first_kernel,
        out_shape=(FIELD, FIELD) + (CELL,) * 6 + (TABLE, X_FACE, X_FACE),
        in_specs=[HBM] * 7,
        out_specs=(VMEM,) * 11,
        scratch_shapes=[
            pltpu.VMEM((16, 16, LANES), jnp.int32),
            pltpu.VMEM((16, 16, LANES), jnp.int32),
            pltpu.SMEM((8,), F32),
            pltpu.SMEM((8,), F32),
            pltpu.SMEM((2,), F32),
            pltpu.SemaphoreType.DMA((7,)),
        ],
        compiler_params=PARAMS,
        name="first",
    )(*(pltpu.with_memory_space_constraint(v, pltpu.HBM) for v in (electric, magnetic, material, absorber_mask, permittivity, conductivity, bloch_phase)))
    state, table, (xa, xb) = out[:8], out[8], out[9:]
    xb = swapped(xb, "gx", 1)
    xa = swapped(xa, "gx", 0)
    out = pl.pallas_call(
        second_kernel,
        out_shape=(FIELD, FIELD) + (CELL,) * 6 + (Y_FACE, Y_FACE),
        in_specs=[VMEM] * 11,
        out_specs=(VMEM,) * 10,
        input_output_aliases={3 + i: i for i in range(8)},
        compiler_params=PARAMS,
        name="second",
    )(xb, xa, table, *state)
    state, (ya, yb) = out[:6], out[8:]
    yb = swapped(yb, "gy", 1)
    ya = swapped(ya, "gy", 0)
    state = pl.pallas_call(
        third_kernel,
        out_shape=(FIELD, FIELD) + (CELL,) * 4,
        in_specs=[VMEM] * 6,
        out_specs=(VMEM,) * 6,
        input_output_aliases={i: i for i in range(6)},
        compiler_params=PARAMS,
        cost_estimate=pl.CostEstimate(flops=20000000000, bytes_accessed=0, transcendentals=0),
        name="third",
    )(*state)
    state = pl.pallas_call(
        fourth_kernel,
        out_shape=(FIELD, FIELD) + (CELL,) * 4,
        in_specs=[VMEM] * 8,
        out_specs=(VMEM,) * 6,
        input_output_aliases={2 + i: i for i in range(6)},
        scratch_shapes=[pltpu.VMEM((XW, 8, LANES), F32), pltpu.VMEM((XW, 8, LANES), F32)],
        compiler_params=PARAMS,
        name="fourth",
    )(ya, table, *state)
    out = pl.pallas_call(
        last_kernel,
        out_shape=(
            jax.ShapeDtypeStruct(electric.shape, F32),
            jax.ShapeDtypeStruct(magnetic.shape, F32),
            FIELD,
            FIELD,
        )
        + (CELL,) * 4,
        in_specs=[VMEM] * 8,
        out_specs=(HBM, HBM) + (VMEM,) * 6,
        input_output_aliases={2 + i: 2 + i for i in range(6)},
        scratch_shapes=[
            pltpu.VMEM((XW, 8, LANES), F32),
            pltpu.VMEM((XW, 8, LANES), F32),
            pltpu.SemaphoreType.DMA((4, 6)),
        ],
        compiler_params=PARAMS,
        name="last",
    )(yb, table, *state)
    return out[0], out[1]


def solution(mesh):
    field = P(None, None, "gx", "gy", None)
    cell = P("gx", "gy", None)
    return jax.shard_map(
        per_device,
        mesh=mesh,
        in_specs=(field, field, cell, cell, P(), P(), P()),
        out_specs=(field, field),
        check_vma=False,
    )
```

```python
import jax
import jax.numpy as jnp
from jax import lax
from jax.experimental import pallas as pl
from jax.experimental.pallas import tpu as pltpu
from jax.sharding import PartitionSpec as P

ABSORB = 10
TIME_STEP = 0.55
ABSORB_PEAK = 1.5

OX, OY = 4, 8
XW, YW = 24, 32
LANES = 128
F32 = jnp.float32

TO_NEXT = (
    ("E", (0, 1, 2), (-3, -2, -1, 16, 17, 18, 19), 15),
    ("H", (0, 1, 2), (-3, -2, -1, 16, 17, 18), 15),
    ("H", (0, 1, 2), (-2, -1, 16, 17, 18), 14),
    ("E", (0, 1, 2), (-1, 16, 17, 18), 14),
    ("H", (0, 2), (16, 17), 13),
)
TO_PREV = (
    ("E", (0, 1, 2), (-4, -3, -2, -1, 16, 17, 18), 0),
    ("H", (0, 1, 2), (-4, -3, -2, -1, 16, 17), 0),
    ("E", (0, 2), (-3, -2, -1, 16), 1),
    ("H", (0, 1, 2), (-3, -2, -1), 1),
)
CELLS_NEXT = tuple((x, 15) for x in (-3, -2, -1, 16, 17, 18)) + tuple((x, 14) for x in (-1, 16, 17))
CELLS_PREV = tuple((x, 0) for x in (-3, -2, -1, 16, 17)) + tuple((x, 1) for x in (-2, -1))

X_TO_NEXT = (
    ("E", (0, 1, 2), (13,), 15),
    ("H", (0,), (13,), 15),
    ("E", (0, 1, 2), (12, 13), 0),
    ("H", (0, 1, 2), (12,), 0),
    ("H", (0,), (13,), 0),
    ("E", (0, 2), (13,), 1),
    ("H", (0,), (13,), 1),
    ("E", (0, 1, 2), (12,), 15),
    ("H", (1, 2), (12,), 15),
    ("E", (0, 1, 2), (13,), 14),
    ("H", (0,), (13,), 14),
)
X_TO_PREV = (
    ("E", (0, 1, 2), (2, 3), 15),
    ("H", (0, 1, 2), (2,), 15),
    ("H", (0, 1, 2), (2,), 14),
    ("E", (0, 1, 2), (2,), 14),
    ("E", (0, 1, 2), (2,), 0),
    ("H", (0, 1, 2), (2,), 0),
)
X_CELLS_NEXT = ((13, 15), (13, 0), (12, 15), (13, 14))
X_CELLS_PREV = ((2, 15), (2, 0))


def entries(face):
    return [(name, c, x, row) for name, comps, columns, row in face for c in comps for x in columns]


LIST_NEXT, LIST_PREV = entries(TO_NEXT), entries(TO_PREV)
HALF = max(len(LIST_NEXT), len(LIST_PREV))
FAR = 16 * 32
Y_ROWS = FAR + -(-(2 * HALF + 2 * max(len(CELLS_NEXT), len(CELLS_PREV))) // 8) * 8

X_LIST_NEXT, X_LIST_PREV = entries(X_TO_NEXT), entries(X_TO_PREV)
X_HALF = max(len(X_LIST_NEXT), len(X_LIST_PREV))
X_SLABS = 32 + -(-(2 * X_HALF + 2 * len(X_CELLS_NEXT)) // 16)


def ghost_row(row):
    return row - 16 if row > 8 else row + 16


def lanes():
    return lax.broadcasted_iota(jnp.int32, (8, LANES), 1)


def ahead(v):
    return jnp.where(lanes() < LANES - 1, pltpu.roll(v, LANES - 1, 1), 0.0)


def behind(v):
    return jnp.where(lanes() > 0, pltpu.roll(v, 1, 1), 0.0)


def row_mask(start, low, high):
    y = lax.broadcasted_iota(jnp.int32, (8, LANES), 0) + (start - OY)
    return (y >= low) & (y < high)


def half_step(field, other, keep, gain, xlow, xhigh, windows, sign):
    along_z = ahead if sign == 1 else behind
    beside = {
        (X, start, p, c): along_z(other[p, c, X, pl.ds(start, 8), :])
        for X in range(xlow + OX, xhigh + OX)
        for start, _, _ in windows
        for p in range(2)
        for c in (1, 0)
    }
    for X in range(xlow + OX, xhigh + OX):
        for start, low, high in windows:
            s, n = pl.ds(start, 8), pl.ds(start + sign, 8)
            whole = low <= start - OY and high >= start - OY + 8
            d, q = keep[X, s, :], gain[X, s, :]
            for p in range(2):
                fx, fy, fz = (other[p, c, X, s, :] for c in range(3))
                y_x, y_z = other[p, 0, X, n, :], other[p, 2, X, n, :]
                x_y, x_z = other[p, 1, X + sign, s, :], other[p, 2, X + sign, s, :]
                curl = (
                    (y_z - fz) - (beside[X, start, p, 1] - fy),
                    (beside[X, start, p, 0] - fx) - (x_z - fz),
                    (x_y - fy) - (y_x - fx),
                )
                for c in range(3):
                    old = field[p, c, X, s, :]
                    new = d * old - q * curl[c]
                    field[p, c, X, s, :] = new if whole else jnp.where(row_mask(start, low, high), new, old)


def half_h(E, H, decay, push, xlow, xhigh, windows):
    half_step(H, E, decay, push, xlow, xhigh, windows, 1)


def half_e(E, H, scale, drive, xlow, xhigh, windows):
    half_step(E, H, scale, drive, xlow, xhigh, windows, -1)


def own(low, high):
    return ((8, low, high), (16, low, high))


SIGMA, X_TURN, Y_TURN = 8, 16, 18


def coefficients(table, material, mask):
    eps = jnp.broadcast_to(table[0:1, :], material.shape)
    sigma = jnp.broadcast_to(table[SIGMA : SIGMA + 1, :], material.shape)
    for m in range(1, 8):
        chosen = material == float(m)
        eps = jnp.where(chosen, table[m : m + 1, :], eps)
        sigma = jnp.where(chosen, table[SIGMA + m : SIGMA + m + 1, :], sigma)
    k = lax.broadcasted_iota(jnp.int32, (1, LANES), 1).astype(F32)
    reach = jnp.maximum(jnp.maximum(ABSORB - k, k - (LANES - 1 - ABSORB)), 0.0) / ABSORB
    magnetic_loss = mask * (ABSORB_PEAK * (reach * reach * reach))
    half = (sigma + magnetic_loss) * (TIME_STEP / 2.0) / eps
    below = 1.0 / (1.0 + half)
    half_m = magnetic_loss * (TIME_STEP / 2.0)
    below_m = 1.0 / (1.0 + half_m)
    return (1.0 - half) * below, (TIME_STEP / eps) * below, (1.0 - half_m) * below_m, TIME_STEP * below_m


def set_coefficients(table, state, X, s, material, mask):
    for ref, value in zip(state, coefficients(table, material, mask)):
        ref[X, s, :] = value


def edge_turn(axis, angle):
    index = lax.axis_index(axis)
    return jnp.where(index == 0, -angle, jnp.where(index == lax.axis_size(axis) - 1, angle, 0.0))


def is_odd(axis):
    return lax.rem(lax.axis_index(axis), 2) == 1


def either(odd, make, a, b):
    pl.when(odd)(lambda: make(b, a))
    pl.when(jnp.logical_not(odd))(lambda: make(a, b))


def turned(table, row, re, im):
    cosine, sine = table[row : row + 1, :], table[row + 1 : row + 2, :]
    return re * cosine - im * sine, re * sine + im * cosine


def pack_y(buf, E, H, mat, mask, rows, extra, items, cells):
    for x in range(16):
        X, base = x + OX, 32 * x
        for p in range(2):
            for c in range(3):
                at = base + 4 * (3 * p + c)
                buf[at : at + 2, :] = E[p, c, X, rows : rows + 2, :]
                buf[at + 2 : at + 4, :] = H[p, c, X, rows : rows + 2, :]
        if extra is not None:
            for p in range(2):
                for i, c in enumerate((0, 2)):
                    at = base + 24 + 2 * p + i
                    buf[at : at + 1, :] = H[p, c, X, extra : extra + 1, :]
        buf[base + 28 : base + 30, :] = mat[X, rows : rows + 2, :]
        buf[base + 30 : base + 32, :] = mask[X, rows : rows + 2, :]

    def put(row, value):
        buf[FAR + row : FAR + row + 1, :] = value

    pack_rows(put, E, H, mat, mask, items, cells, HALF)


def unpack_y(buf, table, E, H, state, mat, mask, below, edge):
    rows, extra, tile = (OY - 2, OY - 3, 0) if below else (OY + 16, None, 24)

    def turn(re, im):
        return turned(table, Y_TURN, re, im) if edge else (re, im)

    for x in range(16):
        X, base = x + OX, 32 * x
        for c in range(3):
            for f, field in enumerate((E, H)):
                at = [base + 4 * (3 * p + c) + 2 * f for p in range(2)]
                re, im = turn(buf[at[0] : at[0] + 2, :], buf[at[1] : at[1] + 2, :])
                field[0, c, X, rows : rows + 2, :] = re
                field[1, c, X, rows : rows + 2, :] = im
        if extra is not None:
            for i, c in enumerate((0, 2)):
                at = base + 24 + i
                re, im = turn(buf[at : at + 1, :], buf[at + 2 : at + 3, :])
                H[0, c, X, extra : extra + 1, :] = re
                H[1, c, X, extra : extra + 1, :] = im
        mat[X, rows - tile : rows - tile + 2, :] = buf[base + 28 : base + 30, :]
        mask[X, rows - tile : rows - tile + 2, :] = buf[base + 30 : base + 32, :]

    def place(x, row):
        return x + OX, ghost_row(row) + OY

    unpack_rows(
        lambda row: buf[FAR + row : FAR + row + 1, :],
        E, H, mat, mask,
        LIST_NEXT if below else LIST_PREV,
        CELLS_NEXT if below else CELLS_PREV,
        HALF, turn, place, tile,
    )
    for X in range(1, XW - 1):
        set_coefficients(table, state, X, pl.ds(tile, 8), mat[X, :, :], mask[X, :, :])


def pack_x(buf, E, H, mat, mask, first, extra, items, cells):
    columns, rows = pl.ds(first + OX, 2), pl.ds(OY, 16)
    for p in range(2):
        for c in range(3):
            at = 2 * (3 * p + c)
            buf[at : at + 2] = E[p, c, columns, rows, :]
            buf[12 + at : 14 + at] = H[p, c, columns, rows, :]
    if extra is not None:
        for p in range(2):
            for i, c in enumerate((1, 2)):
                buf[24 + 2 * p + i] = H[p, c, extra + OX, rows, :]
    buf[28:30] = mat[columns, rows, :]
    buf[30:32] = mask[columns, rows, :]

    def put(row, value):
        buf[32 + row // 16, row % 16 : row % 16 + 1, :] = value

    pack_rows(put, E, H, mat, mask, items, cells, X_HALF)


def pack_rows(put, E, H, mat, mask, items, cells, half):
    for i, (name, c, x, row) in enumerate(items):
        field = E if name == "E" else H
        for p in range(2):
            put(p * half + i, field[p, c, x + OX, row + OY : row + OY + 1, :])
    for i, (x, row) in enumerate(cells):
        put(2 * half + 2 * i, mat[x + OX, row + OY : row + OY + 1, :])
        put(2 * half + 2 * i + 1, mask[x + OX, row + OY : row + OY + 1, :])


def unpack_rows(get, E, H, mat, mask, items, cells, half, turn, place, tile=0):
    for i, (name, c, x, row) in enumerate(items):
        field = E if name == "E" else H
        X, R = place(x, row)
        re, im = turn(get(i), get(half + i))
        field[0, c, X, R : R + 1, :] = re
        field[1, c, X, R : R + 1, :] = im
    for i, (x, row) in enumerate(cells):
        X, R = place(x, row)
        mat[X, R - tile : R - tile + 1, :] = get(2 * half + 2 * i)
        mask[X, R - tile : R - tile + 1, :] = get(2 * half + 2 * i + 1)


SENT_COLUMNS = (0, 1, 2, 12, 13, 14)


def columns_of(source, field, first, count):
    return (
        source.at[:, :, pl.ds(first, count)],
        field.at[:, :, pl.ds(first + OX, count), pl.ds(OY, 16)],
    )


def middle_kernel(
    e_in, h_in, table, e_io, h_io, s_io, d_io, c_io, p_io, m_io, k_io,
    E, H, scale, drive, decay, push, mat, mask,
    sems,
):
    copies = [
        pltpu.make_async_copy(*columns_of(source, field, 4, 8), sems.at[i])
        for i, (source, field) in enumerate(((e_in, E), (h_in, H)))
    ]
    for copy in copies:
        copy.start()
    state = (scale, drive, decay, push)
    for x in range(16):
        if x not in SENT_COLUMNS:
            for start in (8, 16):
                s = pl.ds(start, 8)
                set_coefficients(table, state, x + OX, s, mat[x + OX, s, :], mask[x + OX, s, :])
    for copy in copies:
        copy.wait()
    half_h(E, H, decay, push, 3, 12, own(0, 15))
    half_e(E, H, scale, drive, 3, 13, own(1, 15))
    half_h(E, H, decay, push, 2, 13, own(1, 14))


def first_kernel(
    e_in, h_in, mat_in, mask_in, eps_in, sigma_in, phase_in,
    E, H, scale, drive, decay, push, mat, mask, table, xa, xb,
    raw_mat, raw_mask, eps, sigma, phase, sems,
):
    state = (scale, drive, decay, push)
    pairs = [
        (eps_in, eps),
        (sigma_in, sigma),
        (phase_in, phase),
        (mat_in, raw_mat),
        (mask_in, raw_mask),
    ]
    for columns in ((0, 4), (12, 4)):
        pairs += [columns_of(e_in, E, *columns), columns_of(h_in, H, *columns)]
    copies = [pltpu.make_async_copy(a, b, sems.at[i]) for i, (a, b) in enumerate(pairs)]
    for copy in copies:
        copy.start()
    for copy in copies[:3]:
        copy.wait()
    for m in range(8):
        table[m : m + 1, :] = jnp.full((1, LANES), eps[m], F32)
        table[SIGMA + m : SIGMA + m + 1, :] = jnp.full((1, LANES), sigma[m], F32)
    for axis, row, i in (("gx", X_TURN, 0), ("gy", Y_TURN, 1)):
        angle = jnp.full((1, LANES), edge_turn(axis, phase[i]), F32)
        table[row : row + 1, :] = jnp.cos(angle)
        table[row + 1 : row + 2, :] = jnp.sin(angle)
    copies[3].wait()
    copies[4].wait()
    for x in range(16):
        for start in (0, 8):
            s, t = pl.ds(start, 8), pl.ds(start + OY, 8)
            m, k = raw_mat[x, s, :].astype(F32), raw_mask[x, s, :].astype(F32)
            mat[x + OX, t, :] = m
            mask[x + OX, t, :] = k
            if x in SENT_COLUMNS:
                set_coefficients(table, state, x + OX, t, m, k)
    for copy in copies[5:]:
        copy.wait()

    for low in (0, 12):
        half_h(E, H, decay, push, low, low + 3, own(0, 15))
    for low in (1, 13):
        half_e(E, H, scale, drive, low, low + 2, own(1, 15))
    for low in (1, 13):
        half_h(E, H, decay, push, low, low + 1, own(1, 14))

    def x_faces(to_next, to_prev):
        pack_x(to_next, E, H, mat, mask, 14, 13, X_LIST_NEXT, X_CELLS_NEXT)
        pack_x(to_prev, E, H, mat, mask, 0, None, X_LIST_PREV, X_CELLS_PREV)

    either(is_odd("gx"), x_faces, xa, xb)


def second_kernel(
    xb, xa, table, e_io, h_io, s_io, d_io, c_io, p_io, m_io, k_io,
    E, H, scale, drive, decay, push, mat, mask, ya, yb,
):
    state = (scale, drive, decay, push)
    rows = pl.ds(OY, 16)

    def place(buf, first, extra, items, cells, shift, edge):
        def turn(re, im):
            return turned(table, X_TURN, re, im) if edge else (re, im)

        for field, base in ((E, 0), (H, 12)):
            for c in range(3):
                at = base + 2 * c
                for j in range(2):
                    re, im = turn(buf[at + j], buf[at + 6 + j])
                    field[0, c, first + OX + j, rows, :] = re
                    field[1, c, first + OX + j, rows, :] = im
        if extra is not None:
            for i, c in enumerate((1, 2)):
                re, im = turn(buf[24 + i], buf[26 + i])
                H[0, c, extra + OX, rows, :] = re
                H[1, c, extra + OX, rows, :] = im
        for j in range(2):
            X = first + OX + j
            for start in (0, 8):
                s, t = pl.ds(start, 8), pl.ds(start + OY, 8)
                m, k = buf[28 + j, s, :], buf[30 + j, s, :]
                mat[X, t, :] = m
                mask[X, t, :] = k
                set_coefficients(table, state, X, t, m, k)

        def get(row):
            return buf[32 + row // 16, row % 16 : row % 16 + 1, :]

        unpack_rows(
            get, E, H, mat, mask, items, cells, X_HALF, turn, lambda x, row: (x + shift + OX, row + OY)
        )

    def ghosts(above, below, odd):
        place(below, -2, -3, X_LIST_NEXT, X_CELLS_NEXT, -16, not odd)
        place(above, 16, None, X_LIST_PREV, X_CELLS_PREV, 16, odd)

    gx_odd = is_odd("gx")
    pl.when(gx_odd)(lambda: ghosts(xb, xa, True))
    pl.when(jnp.logical_not(gx_odd))(lambda: ghosts(xa, xb, False))

    for X in (0, 1, 22):
        for start in (8, 16):
            s = pl.ds(start, 8)
            set_coefficients(table, state, X, s, mat[X, s, :], mask[X, s, :])

    half_h(E, H, decay, push, -1, 0, own(0, 15))
    half_h(E, H, decay, push, 15, 16, own(0, 15))
    half_e(E, H, scale, drive, -1, 1, own(1, 15))
    half_e(E, H, scale, drive, 15, 17, own(1, 15))
    half_h(E, H, decay, push, -2, 1, own(1, 14))
    half_h(E, H, decay, push, 14, 17, own(1, 14))

    def pack(to_next, to_prev):
        pack_y(to_next, E, H, mat, mask, OY + 14, OY + 13, LIST_NEXT, CELLS_NEXT)
        pack_y(to_prev, E, H, mat, mask, OY, None, LIST_PREV, CELLS_PREV)

    either(is_odd("gy"), pack, ya, yb)


def third_kernel(
    e_io, h_io, s_io, d_io, c_io, p_io,
    E, H, scale, drive, decay, push,
):
    half_e(E, H, scale, drive, -2, 18, own(2, 14))
    half_h(E, H, decay, push, -2, 17, own(2, 13))
    half_e(E, H, scale, drive, -1, 17, own(3, 13))
    half_h(E, H, decay, push, -1, 16, own(3, 12))
    half_e(E, H, scale, drive, 0, 16, own(4, 12))


def fourth_kernel(
    ya, table, e_io, h_io, s_io, d_io, c_io, p_io,
    E, H, scale, drive, decay, push,
    mat, mask,
):
    gy_odd = is_odd("gy")
    args = (ya, table, E, H, (scale, drive, decay, push), mat, mask)
    pl.when(gy_odd)(lambda: unpack_y(*args, True, False))
    pl.when(jnp.logical_not(gy_odd))(lambda: unpack_y(*args, False, False))


def last_kernel(
    yb, table, e_io, h_io, s_io, d_io, c_io, p_io,
    e_out, h_out, E, H, scale, drive, decay, push,
    mat, mask, sems,
):
    gy_odd = is_odd("gy")
    args = (yb, table, E, H, (scale, drive, decay, push), mat, mask)
    pl.when(gy_odd)(lambda: unpack_y(*args, False, True))
    pl.when(jnp.logical_not(gy_odd))(lambda: unpack_y(*args, True, True))

    def sides(low, low_end, high, high_end):
        return ((4, low, low_end), (20, high, high_end))

    copies = []
    for part, (start, end) in enumerate(((None, 8), (8, 16))):

        def span(low, shift, high, start=start, end=end):
            return low if start is None else start + shift, high if end == 16 else end + shift

        half_h(E, H, decay, push, *span(-4, 3, 19), sides(-1, 0, 15, 16))
        half_e(E, H, scale, drive, *span(-3, 3, 19), sides(-1, 1, 15, 17))
        half_h(E, H, decay, push, *span(-3, 2, 18), sides(-2, 1, 14, 17))
        half_e(E, H, scale, drive, *span(-2, 2, 18), sides(-2, 2, 14, 18))
        half_h(E, H, decay, push, *span(-2, 1, 17), sides(-2, 2, 13, 17))
        half_e(E, H, scale, drive, *span(-1, 1, 17), sides(-1, 3, 13, 17))
        half_h(E, H, decay, push, *span(-1, 0, 16), sides(-1, 3, 12, 16))
        copies += copy_out(H, h_out, sems.at[2 * part], end - 8)
        half_e(E, H, scale, drive, *span(0, 0, 16), sides(0, 4, 12, 16))
        copies += copy_out(E, e_out, sems.at[2 * part + 1], end - 8)
    for copy in copies:
        copy.wait()


def copy_out(field, out, sem, first):
    copies = []
    for p in range(2):
        for c in range(3):
            copy = pltpu.make_async_copy(
                field.at[p, c, pl.ds(first + OX, 8), pl.ds(OY, 16)], out.at[p, c, pl.ds(first, 8)], sem.at[3 * p + c]
            )
            copy.start()
            copies.append(copy)
    return copies


VMEM = pl.BlockSpec(memory_space=pltpu.VMEM)
HBM = pl.BlockSpec(memory_space=pltpu.HBM)
FIELD = jax.ShapeDtypeStruct((2, 3, XW, YW, LANES), F32)
CELL = jax.ShapeDtypeStruct((XW, YW, LANES), F32)
TABLE = jax.ShapeDtypeStruct((24, LANES), F32)
X_FACE = jax.ShapeDtypeStruct((X_SLABS, 16, LANES), F32)
Y_FACE = jax.ShapeDtypeStruct((Y_ROWS, LANES), F32)
PARAMS = pltpu.CompilerParams(vmem_limit_bytes=32 * 1024 * 1024)


def swapped(value, axis, odd):
    count = lax.axis_size(axis)
    pairs = []
    for low in range(odd, count, 2):
        high = (low + 1) % count
        pairs += [(low, high), (high, low)]
    return lax.ppermute(value, axis, pairs)


def in_hbm(values):
    return tuple(pltpu.with_memory_space_constraint(v, pltpu.HBM) for v in values)


def per_device(electric, magnetic, material, absorber_mask, permittivity, conductivity, bloch_phase):
    electric, magnetic = in_hbm((electric, magnetic))
    out = pl.pallas_call(
        first_kernel,
        out_shape=(FIELD, FIELD) + (CELL,) * 6 + (TABLE, X_FACE, X_FACE),
        in_specs=[HBM] * 7,
        out_specs=(VMEM,) * 11,
        scratch_shapes=[
            pltpu.VMEM((16, 16, LANES), jnp.int32),
            pltpu.VMEM((16, 16, LANES), jnp.int32),
            pltpu.SMEM((8,), F32),
            pltpu.SMEM((8,), F32),
            pltpu.SMEM((2,), F32),
            pltpu.SemaphoreType.DMA((9,)),
        ],
        compiler_params=PARAMS,
        name="first",
    )(electric, magnetic, *in_hbm((material, absorber_mask, permittivity, conductivity, bloch_phase)))
    state, table, (xa, xb) = out[:8], out[8], out[9:]
    xb = swapped(xb, "gx", 1)
    xa = swapped(xa, "gx", 0)
    state = pl.pallas_call(
        middle_kernel,
        out_shape=(FIELD, FIELD) + (CELL,) * 6,
        in_specs=[HBM] * 2 + [VMEM] * 9,
        out_specs=(VMEM,) * 8,
        input_output_aliases={3 + i: i for i in range(8)},
        scratch_shapes=[pltpu.SemaphoreType.DMA((2,))],
        cost_estimate=pl.CostEstimate(flops=10000000000, bytes_accessed=0, transcendentals=0),
        compiler_params=PARAMS,
        name="middle",
    )(electric, magnetic, table, *state)
    out = pl.pallas_call(
        second_kernel,
        out_shape=(FIELD, FIELD) + (CELL,) * 6 + (Y_FACE, Y_FACE),
        in_specs=[VMEM] * 11,
        out_specs=(VMEM,) * 10,
        input_output_aliases={3 + i: i for i in range(8)},
        compiler_params=PARAMS,
        name="second",
    )(xb, xa, table, *state)
    state, (ya, yb) = out[:6], out[8:]
    yb = swapped(yb, "gy", 1)
    ya = swapped(ya, "gy", 0)
    state = pl.pallas_call(
        third_kernel,
        out_shape=(FIELD, FIELD) + (CELL,) * 4,
        in_specs=[VMEM] * 6,
        out_specs=(VMEM,) * 6,
        input_output_aliases={i: i for i in range(6)},
        compiler_params=PARAMS,
        cost_estimate=pl.CostEstimate(flops=20000000000, bytes_accessed=0, transcendentals=0),
        name="third",
    )(*state)
    state = pl.pallas_call(
        fourth_kernel,
        out_shape=(FIELD, FIELD) + (CELL,) * 4,
        in_specs=[VMEM] * 8,
        out_specs=(VMEM,) * 6,
        input_output_aliases={2 + i: i for i in range(6)},
        scratch_shapes=[pltpu.VMEM((XW, 8, LANES), F32), pltpu.VMEM((XW, 8, LANES), F32)],
        compiler_params=PARAMS,
        name="fourth",
    )(ya, table, *state)
    out = pl.pallas_call(
        last_kernel,
        out_shape=(
            jax.ShapeDtypeStruct(electric.shape, F32),
            jax.ShapeDtypeStruct(magnetic.shape, F32),
            FIELD,
            FIELD,
        )
        + (CELL,) * 4,
        in_specs=[VMEM] * 8,
        out_specs=(HBM, HBM) + (VMEM,) * 6,
        input_output_aliases={2 + i: 2 + i for i in range(6)},
        scratch_shapes=[
            pltpu.VMEM((XW, 8, LANES), F32),
            pltpu.VMEM((XW, 8, LANES), F32),
            pltpu.SemaphoreType.DMA((4, 6)),
        ],
        compiler_params=PARAMS,
        name="last",
    )(yb, table, *state)
    return out[0], out[1]


def solution(mesh):
    field = P(None, None, "gx", "gy", None)
    cell = P("gx", "gy", None)
    return jax.shard_map(
        per_device,
        mesh=mesh,
        in_specs=(field, field, cell, cell, P(), P(), P()),
        out_specs=(field, field),
        check_vma=False,
    )
```

```python
import jax
import jax.numpy as jnp
from jax import lax
from jax.experimental import pallas as pl
from jax.experimental.pallas import tpu as pltpu
from jax.sharding import PartitionSpec as P

ABSORB = 10
TIME_STEP = 0.55
ABSORB_PEAK = 1.5

OX, OY = 4, 8
XW, YW = 24, 32
LANES = 128
F32 = jnp.float32

TO_NEXT = (
    ("E", (0, 1, 2), (-3, -2, -1, 16, 17, 18, 19), 15),
    ("H", (0, 1, 2), (-3, -2, -1, 16, 17, 18), 15),
    ("H", (0, 1, 2), (-2, -1, 16, 17, 18), 14),
    ("E", (0, 1, 2), (-1, 16, 17, 18), 14),
    ("H", (0, 2), (16, 17), 13),
)
TO_PREV = (
    ("E", (0, 1, 2), (-4, -3, -2, -1, 16, 17, 18), 0),
    ("H", (0, 1, 2), (-4, -3, -2, -1, 16, 17), 0),
    ("E", (0, 2), (-3, -2, -1, 16), 1),
    ("H", (0, 1, 2), (-3, -2, -1), 1),
)
CELLS_NEXT = tuple((x, 15) for x in (-3, -2, -1, 16, 17, 18)) + tuple((x, 14) for x in (-1, 16, 17))
CELLS_PREV = tuple((x, 0) for x in (-3, -2, -1, 16, 17)) + tuple((x, 1) for x in (-2, -1))

X_TO_NEXT = (
    ("E", (0, 1, 2), (13,), 15),
    ("H", (0,), (13,), 15),
    ("E", (0, 1, 2), (12, 13), 0),
    ("H", (0, 1, 2), (12,), 0),
    ("H", (0,), (13,), 0),
    ("E", (0, 2), (13,), 1),
    ("H", (0,), (13,), 1),
    ("E", (0, 1, 2), (12,), 15),
    ("H", (1, 2), (12,), 15),
    ("E", (0, 1, 2), (13,), 14),
    ("H", (0,), (13,), 14),
)
X_TO_PREV = (
    ("E", (0, 1, 2), (2, 3), 15),
    ("H", (0, 1, 2), (2,), 15),
    ("H", (0, 1, 2), (2,), 14),
    ("E", (0, 1, 2), (2,), 14),
    ("E", (0, 1, 2), (2,), 0),
    ("H", (0, 1, 2), (2,), 0),
)
X_CELLS_NEXT = ((13, 15), (13, 0), (12, 15), (13, 14))
X_CELLS_PREV = ((2, 15), (2, 0))


def entries(face):
    return [(name, c, x, row) for name, comps, columns, row in face for c in comps for x in columns]


LIST_NEXT, LIST_PREV = entries(TO_NEXT), entries(TO_PREV)
HALF = max(len(LIST_NEXT), len(LIST_PREV))
FAR = 16 * 32
Y_ROWS = FAR + -(-(2 * HALF + 2 * max(len(CELLS_NEXT), len(CELLS_PREV))) // 8) * 8

X_LIST_NEXT, X_LIST_PREV = entries(X_TO_NEXT), entries(X_TO_PREV)
X_HALF = max(len(X_LIST_NEXT), len(X_LIST_PREV))
X_SLABS = 32 + -(-(2 * X_HALF + 2 * len(X_CELLS_NEXT)) // 16)


def ghost_row(row):
    return row - 16 if row > 8 else row + 16


def lanes():
    return lax.broadcasted_iota(jnp.int32, (8, LANES), 1)


def ahead(v):
    return jnp.where(lanes() < LANES - 1, pltpu.roll(v, LANES - 1, 1), 0.0)


def behind(v):
    return jnp.where(lanes() > 0, pltpu.roll(v, 1, 1), 0.0)


def row_mask(start, low, high):
    y = lax.broadcasted_iota(jnp.int32, (8, LANES), 0) + (start - OY)
    return (y >= low) & (y < high)


def half_step(field, other, keep, gain, xlow, xhigh, windows, sign):
    along_z = ahead if sign == 1 else behind
    beside = {
        (X, start, p, c): along_z(other[p, c, X, pl.ds(start, 8), :])
        for X in range(xlow + OX, xhigh + OX)
        for start, _, _ in windows
        for p in range(2)
        for c in (1, 0)
    }
    for X in range(xlow + OX, xhigh + OX):
        for start, low, high in windows:
            s, n = pl.ds(start, 8), pl.ds(start + sign, 8)
            whole = low <= start - OY and high >= start - OY + 8
            d, q = keep[X, s, :], gain[X, s, :]
            for p in range(2):
                fx, fy, fz = (other[p, c, X, s, :] for c in range(3))
                y_x, y_z = other[p, 0, X, n, :], other[p, 2, X, n, :]
                x_y, x_z = other[p, 1, X + sign, s, :], other[p, 2, X + sign, s, :]
                curl = (
                    (y_z - fz) - (beside[X, start, p, 1] - fy),
                    (beside[X, start, p, 0] - fx) - (x_z - fz),
                    (x_y - fy) - (y_x - fx),
                )
                for c in range(3):
                    old = field[p, c, X, s, :]
                    new = d * old - q * curl[c]
                    field[p, c, X, s, :] = new if whole else jnp.where(row_mask(start, low, high), new, old)


def half_h(E, H, decay, push, xlow, xhigh, windows):
    half_step(H, E, decay, push, xlow, xhigh, windows, 1)


def half_e(E, H, scale, drive, xlow, xhigh, windows):
    half_step(E, H, scale, drive, xlow, xhigh, windows, -1)


def own(low, high):
    return ((8, low, high), (16, low, high))


SIGMA, X_TURN, Y_TURN = 8, 16, 18


def coefficients(table, material, mask):
    eps = jnp.broadcast_to(table[0:1, :], material.shape)
    sigma = jnp.broadcast_to(table[SIGMA : SIGMA + 1, :], material.shape)
    for m in range(1, 8):
        chosen = material == float(m)
        eps = jnp.where(chosen, table[m : m + 1, :], eps)
        sigma = jnp.where(chosen, table[SIGMA + m : SIGMA + m + 1, :], sigma)
    k = lax.broadcasted_iota(jnp.int32, (1, LANES), 1).astype(F32)
    reach = jnp.maximum(jnp.maximum(ABSORB - k, k - (LANES - 1 - ABSORB)), 0.0) / ABSORB
    magnetic_loss = mask * (ABSORB_PEAK * (reach * reach * reach))
    half = (sigma + magnetic_loss) * (TIME_STEP / 2.0) / eps
    below = 1.0 / (1.0 + half)
    half_m = magnetic_loss * (TIME_STEP / 2.0)
    below_m = 1.0 / (1.0 + half_m)
    return (1.0 - half) * below, (TIME_STEP / eps) * below, (1.0 - half_m) * below_m, TIME_STEP * below_m


def set_coefficients(table, state, X, s, material, mask):
    for ref, value in zip(state, coefficients(table, material, mask)):
        ref[X, s, :] = value


def edge_turn(axis, angle):
    index = lax.axis_index(axis)
    return jnp.where(index == 0, -angle, jnp.where(index == lax.axis_size(axis) - 1, angle, 0.0))


def is_odd(axis):
    return lax.rem(lax.axis_index(axis), 2) == 1


def either(odd, make, a, b):
    pl.when(odd)(lambda: make(b, a))
    pl.when(jnp.logical_not(odd))(lambda: make(a, b))


def turned(table, row, re, im):
    cosine, sine = table[row : row + 1, :], table[row + 1 : row + 2, :]
    return re * cosine - im * sine, re * sine + im * cosine


def pack_y(buf, E, H, mat, mask, rows, extra, columns):
    for x in columns:
        X, base = x + OX, 32 * x
        for p in range(2):
            for c in range(3):
                at = base + 4 * (3 * p + c)
                buf[at : at + 2, :] = E[p, c, X, rows : rows + 2, :]
                buf[at + 2 : at + 4, :] = H[p, c, X, rows : rows + 2, :]
        if extra is not None:
            for p in range(2):
                for i, c in enumerate((0, 2)):
                    at = base + 24 + 2 * p + i
                    buf[at : at + 1, :] = H[p, c, X, extra : extra + 1, :]
        buf[base + 28 : base + 30, :] = mat[X, rows : rows + 2, :]
        buf[base + 30 : base + 32, :] = mask[X, rows : rows + 2, :]


def pack_far(buf, E, H, mat, mask, items, cells):
    def put(row, value):
        buf[FAR + row : FAR + row + 1, :] = value

    pack_rows(put, E, H, mat, mask, items, cells, HALF)


def unpack_y(buf, table, E, H, state, mat, mask, below, edge):
    rows, extra, tile = (OY - 2, OY - 3, 0) if below else (OY + 16, None, 24)

    def turn(re, im):
        return turned(table, Y_TURN, re, im) if edge else (re, im)

    for x in range(16):
        X, base = x + OX, 32 * x
        for c in range(3):
            for f, field in enumerate((E, H)):
                at = [base + 4 * (3 * p + c) + 2 * f for p in range(2)]
                re, im = turn(buf[at[0] : at[0] + 2, :], buf[at[1] : at[1] + 2, :])
                field[0, c, X, rows : rows + 2, :] = re
                field[1, c, X, rows : rows + 2, :] = im
        if extra is not None:
            for i, c in enumerate((0, 2)):
                at = base + 24 + i
                re, im = turn(buf[at : at + 1, :], buf[at + 2 : at + 3, :])
                H[0, c, X, extra : extra + 1, :] = re
                H[1, c, X, extra : extra + 1, :] = im
        mat[X, rows - tile : rows - tile + 2, :] = buf[base + 28 : base + 30, :]
        mask[X, rows - tile : rows - tile + 2, :] = buf[base + 30 : base + 32, :]

    def place(x, row):
        return x + OX, ghost_row(row) + OY

    unpack_rows(
        lambda row: buf[FAR + row : FAR + row + 1, :],
        E, H, mat, mask,
        LIST_NEXT if below else LIST_PREV,
        CELLS_NEXT if below else CELLS_PREV,
        HALF, turn, place, tile,
    )
    for X in range(1, XW - 1):
        set_coefficients(table, state, X, pl.ds(tile, 8), mat[X, :, :], mask[X, :, :])


def pack_x(buf, E, H, mat, mask, first, extra, items, cells):
    columns, rows = pl.ds(first + OX, 2), pl.ds(OY, 16)
    for p in range(2):
        for c in range(3):
            at = 2 * (3 * p + c)
            buf[at : at + 2] = E[p, c, columns, rows, :]
            buf[12 + at : 14 + at] = H[p, c, columns, rows, :]
    if extra is not None:
        for p in range(2):
            for i, c in enumerate((1, 2)):
                buf[24 + 2 * p + i] = H[p, c, extra + OX, rows, :]
    buf[28:30] = mat[columns, rows, :]
    buf[30:32] = mask[columns, rows, :]

    def put(row, value):
        buf[32 + row // 16, row % 16 : row % 16 + 1, :] = value

    pack_rows(put, E, H, mat, mask, items, cells, X_HALF)


def pack_rows(put, E, H, mat, mask, items, cells, half):
    for i, (name, c, x, row) in enumerate(items):
        field = E if name == "E" else H
        for p in range(2):
            put(p * half + i, field[p, c, x + OX, row + OY : row + OY + 1, :])
    for i, (x, row) in enumerate(cells):
        put(2 * half + 2 * i, mat[x + OX, row + OY : row + OY + 1, :])
        put(2 * half + 2 * i + 1, mask[x + OX, row + OY : row + OY + 1, :])


def unpack_rows(get, E, H, mat, mask, items, cells, half, turn, place, tile=0):
    for i, (name, c, x, row) in enumerate(items):
        field = E if name == "E" else H
        X, R = place(x, row)
        re, im = turn(get(i), get(half + i))
        field[0, c, X, R : R + 1, :] = re
        field[1, c, X, R : R + 1, :] = im
    for i, (x, row) in enumerate(cells):
        X, R = place(x, row)
        mat[X, R - tile : R - tile + 1, :] = get(2 * half + 2 * i)
        mask[X, R - tile : R - tile + 1, :] = get(2 * half + 2 * i + 1)


SENT_COLUMNS = (0, 1, 2, 12, 13, 14)


def columns_of(source, field, first, count):
    return (
        source.at[:, :, pl.ds(first, count)],
        field.at[:, :, pl.ds(first + OX, count), pl.ds(OY, 16)],
    )


def middle_kernel(
    e_in, h_in, table, e_io, h_io, s_io, d_io, c_io, p_io, m_io, k_io,
    E, H, scale, drive, decay, push, mat, mask, ya, yb,
    sems,
):
    copies = [
        pltpu.make_async_copy(*columns_of(source, field, 4, 8), sems.at[i])
        for i, (source, field) in enumerate(((e_in, E), (h_in, H)))
    ]
    for copy in copies:
        copy.start()
    state = (scale, drive, decay, push)
    for x in range(16):
        if x not in SENT_COLUMNS:
            for start in (8, 16):
                s = pl.ds(start, 8)
                set_coefficients(table, state, x + OX, s, mat[x + OX, s, :], mask[x + OX, s, :])
    for copy in copies:
        copy.wait()
    half_h(E, H, decay, push, 3, 12, own(0, 15))
    half_e(E, H, scale, drive, 3, 13, own(1, 15))
    half_h(E, H, decay, push, 2, 13, own(1, 14))

    def pack(to_next, to_prev):
        pack_y(to_next, E, H, mat, mask, OY + 14, OY + 13, range(1, 14))
        pack_y(to_prev, E, H, mat, mask, OY, None, range(1, 14))

    either(is_odd("gy"), pack, ya, yb)


def first_kernel(
    e_in, h_in, mat_in, mask_in, eps_in, sigma_in, phase_in,
    E, H, scale, drive, decay, push, mat, mask, table, xa, xb,
    raw_mat, raw_mask, eps, sigma, phase, sems,
):
    state = (scale, drive, decay, push)
    pairs = [
        (eps_in, eps),
        (sigma_in, sigma),
        (phase_in, phase),
        (mat_in, raw_mat),
        (mask_in, raw_mask),
    ]
    for columns in ((0, 4), (12, 4)):
        pairs += [columns_of(e_in, E, *columns), columns_of(h_in, H, *columns)]
    copies = [pltpu.make_async_copy(a, b, sems.at[i]) for i, (a, b) in enumerate(pairs)]
    for copy in copies:
        copy.start()
    for copy in copies[:3]:
        copy.wait()
    for m in range(8):
        table[m : m + 1, :] = jnp.full((1, LANES), eps[m], F32)
        table[SIGMA + m : SIGMA + m + 1, :] = jnp.full((1, LANES), sigma[m], F32)
    for axis, row, i in (("gx", X_TURN, 0), ("gy", Y_TURN, 1)):
        angle = jnp.full((1, LANES), edge_turn(axis, phase[i]), F32)
        table[row : row + 1, :] = jnp.cos(angle)
        table[row + 1 : row + 2, :] = jnp.sin(angle)
    copies[3].wait()
    copies[4].wait()
    for x in range(16):
        for start in (0, 8):
            s, t = pl.ds(start, 8), pl.ds(start + OY, 8)
            m, k = raw_mat[x, s, :].astype(F32), raw_mask[x, s, :].astype(F32)
            mat[x + OX, t, :] = m
            mask[x + OX, t, :] = k
            if x in SENT_COLUMNS:
                set_coefficients(table, state, x + OX, t, m, k)
    for copy in copies[5:]:
        copy.wait()

    for low in (0, 12):
        half_h(E, H, decay, push, low, low + 3, own(0, 15))
    for low in (1, 13):
        half_e(E, H, scale, drive, low, low + 2, own(1, 15))
    for low in (1, 13):
        half_h(E, H, decay, push, low, low + 1, own(1, 14))

    def x_faces(to_next, to_prev):
        pack_x(to_next, E, H, mat, mask, 14, 13, X_LIST_NEXT, X_CELLS_NEXT)
        pack_x(to_prev, E, H, mat, mask, 0, None, X_LIST_PREV, X_CELLS_PREV)

    either(is_odd("gx"), x_faces, xa, xb)


def second_kernel(
    xb, xa, table, e_io, h_io, s_io, d_io, c_io, p_io, m_io, k_io, ya_io, yb_io,
    E, H, scale, drive, decay, push, mat, mask, ya, yb,
):
    state = (scale, drive, decay, push)
    rows = pl.ds(OY, 16)

    def place(buf, first, extra, items, cells, shift, edge):
        def turn(re, im):
            return turned(table, X_TURN, re, im) if edge else (re, im)

        for field, base in ((E, 0), (H, 12)):
            for c in range(3):
                at = base + 2 * c
                for j in range(2):
                    re, im = turn(buf[at + j], buf[at + 6 + j])
                    field[0, c, first + OX + j, rows, :] = re
                    field[1, c, first + OX + j, rows, :] = im
        if extra is not None:
            for i, c in enumerate((1, 2)):
                re, im = turn(buf[24 + i], buf[26 + i])
                H[0, c, extra + OX, rows, :] = re
                H[1, c, extra + OX, rows, :] = im
        for j in range(2):
            X = first + OX + j
            for start in (0, 8):
                s, t = pl.ds(start, 8), pl.ds(start + OY, 8)
                m, k = buf[28 + j, s, :], buf[30 + j, s, :]
                mat[X, t, :] = m
                mask[X, t, :] = k
                set_coefficients(table, state, X, t, m, k)

        def get(row):
            return buf[32 + row // 16, row % 16 : row % 16 + 1, :]

        unpack_rows(
            get, E, H, mat, mask, items, cells, X_HALF, turn, lambda x, row: (x + shift + OX, row + OY)
        )

    def ghosts(above, below, odd):
        place(below, -2, -3, X_LIST_NEXT, X_CELLS_NEXT, -16, not odd)
        place(above, 16, None, X_LIST_PREV, X_CELLS_PREV, 16, odd)

    gx_odd = is_odd("gx")
    pl.when(gx_odd)(lambda: ghosts(xb, xa, True))
    pl.when(jnp.logical_not(gx_odd))(lambda: ghosts(xa, xb, False))

    for X in (0, 1, 22):
        for start in (8, 16):
            s = pl.ds(start, 8)
            set_coefficients(table, state, X, s, mat[X, s, :], mask[X, s, :])

    half_h(E, H, decay, push, -1, 0, own(0, 15))
    half_h(E, H, decay, push, 15, 16, own(0, 15))
    half_e(E, H, scale, drive, -1, 1, own(1, 15))
    half_e(E, H, scale, drive, 15, 17, own(1, 15))
    half_h(E, H, decay, push, -2, 1, own(1, 14))
    half_h(E, H, decay, push, 14, 17, own(1, 14))

    def pack(to_next, to_prev):
        pack_y(to_next, E, H, mat, mask, OY + 14, OY + 13, (0, 14, 15))
        pack_far(to_next, E, H, mat, mask, LIST_NEXT, CELLS_NEXT)
        pack_y(to_prev, E, H, mat, mask, OY, None, (0, 14, 15))
        pack_far(to_prev, E, H, mat, mask, LIST_PREV, CELLS_PREV)

    either(is_odd("gy"), pack, ya, yb)


def third_kernel(
    e_io, h_io, s_io, d_io, c_io, p_io,
    E, H, scale, drive, decay, push,
):
    half_e(E, H, scale, drive, -2, 18, own(2, 14))
    half_h(E, H, decay, push, -2, 17, own(2, 13))
    half_e(E, H, scale, drive, -1, 17, own(3, 13))
    half_h(E, H, decay, push, -1, 16, own(3, 12))
    half_e(E, H, scale, drive, 0, 16, own(4, 12))


def fourth_kernel(
    ya, table, e_io, h_io, s_io, d_io, c_io, p_io,
    E, H, scale, drive, decay, push,
    mat, mask,
):
    gy_odd = is_odd("gy")
    args = (ya, table, E, H, (scale, drive, decay, push), mat, mask)
    pl.when(gy_odd)(lambda: unpack_y(*args, True, False))
    pl.when(jnp.logical_not(gy_odd))(lambda: unpack_y(*args, False, False))


def last_kernel(
    yb, table, e_io, h_io, s_io, d_io, c_io, p_io,
    e_out, h_out, E, H, scale, drive, decay, push,
    mat, mask, sems,
):
    gy_odd = is_odd("gy")
    args = (yb, table, E, H, (scale, drive, decay, push), mat, mask)
    pl.when(gy_odd)(lambda: unpack_y(*args, False, True))
    pl.when(jnp.logical_not(gy_odd))(lambda: unpack_y(*args, True, True))

    def sides(low, low_end, high, high_end):
        return ((4, low, low_end), (20, high, high_end))

    copies = []
    for part, (start, end) in enumerate(((None, 8), (8, 16))):

        def span(low, shift, high, start=start, end=end):
            return low if start is None else start + shift, high if end == 16 else end + shift

        half_h(E, H, decay, push, *span(-4, 3, 19), sides(-1, 0, 15, 16))
        half_e(E, H, scale, drive, *span(-3, 3, 19), sides(-1, 1, 15, 17))
        half_h(E, H, decay, push, *span(-3, 2, 18), sides(-2, 1, 14, 17))
        half_e(E, H, scale, drive, *span(-2, 2, 18), sides(-2, 2, 14, 18))
        half_h(E, H, decay, push, *span(-2, 1, 17), sides(-2, 2, 13, 17))
        half_e(E, H, scale, drive, *span(-1, 1, 17), sides(-1, 3, 13, 17))
        half_h(E, H, decay, push, *span(-1, 0, 16), sides(-1, 3, 12, 16))
        copies += copy_out(H, h_out, sems.at[2 * part], end - 8)
        half_e(E, H, scale, drive, *span(0, 0, 16), sides(0, 4, 12, 16))
        copies += copy_out(E, e_out, sems.at[2 * part + 1], end - 8)
    for copy in copies:
        copy.wait()


def copy_out(field, out, sem, first):
    copies = []
    for p in range(2):
        for c in range(3):
            copy = pltpu.make_async_copy(
                field.at[p, c, pl.ds(first + OX, 8), pl.ds(OY, 16)], out.at[p, c, pl.ds(first, 8)], sem.at[3 * p + c]
            )
            copy.start()
            copies.append(copy)
    return copies


VMEM = pl.BlockSpec(memory_space=pltpu.VMEM)
HBM = pl.BlockSpec(memory_space=pltpu.HBM)
FIELD = jax.ShapeDtypeStruct((2, 3, XW, YW, LANES), F32)
CELL = jax.ShapeDtypeStruct((XW, YW, LANES), F32)
TABLE = jax.ShapeDtypeStruct((24, LANES), F32)
X_FACE = jax.ShapeDtypeStruct((X_SLABS, 16, LANES), F32)
Y_FACE = jax.ShapeDtypeStruct((Y_ROWS, LANES), F32)
PARAMS = pltpu.CompilerParams(vmem_limit_bytes=32 * 1024 * 1024)


def swapped(value, axis, odd):
    count = lax.axis_size(axis)
    pairs = []
    for low in range(odd, count, 2):
        high = (low + 1) % count
        pairs += [(low, high), (high, low)]
    return lax.ppermute(value, axis, pairs)


def in_hbm(values):
    return tuple(pltpu.with_memory_space_constraint(v, pltpu.HBM) for v in values)


def per_device(electric, magnetic, material, absorber_mask, permittivity, conductivity, bloch_phase):
    electric, magnetic = in_hbm((electric, magnetic))
    out = pl.pallas_call(
        first_kernel,
        out_shape=(FIELD, FIELD) + (CELL,) * 6 + (TABLE, X_FACE, X_FACE),
        in_specs=[HBM] * 7,
        out_specs=(VMEM,) * 11,
        scratch_shapes=[
            pltpu.VMEM((16, 16, LANES), jnp.int32),
            pltpu.VMEM((16, 16, LANES), jnp.int32),
            pltpu.SMEM((8,), F32),
            pltpu.SMEM((8,), F32),
            pltpu.SMEM((2,), F32),
            pltpu.SemaphoreType.DMA((9,)),
        ],
        compiler_params=PARAMS,
        name="first",
    )(electric, magnetic, *in_hbm((material, absorber_mask, permittivity, conductivity, bloch_phase)))
    state, table, (xa, xb) = out[:8], out[8], out[9:]
    xb = swapped(xb, "gx", 1)
    xa = swapped(xa, "gx", 0)
    state = pl.pallas_call(
        middle_kernel,
        out_shape=(FIELD, FIELD) + (CELL,) * 6 + (Y_FACE, Y_FACE),
        in_specs=[HBM] * 2 + [VMEM] * 9,
        out_specs=(VMEM,) * 10,
        input_output_aliases={3 + i: i for i in range(8)},
        scratch_shapes=[pltpu.SemaphoreType.DMA((2,))],
        cost_estimate=pl.CostEstimate(flops=10000000000, bytes_accessed=0, transcendentals=0),
        compiler_params=PARAMS,
        name="middle",
    )(electric, magnetic, table, *state)
    out = pl.pallas_call(
        second_kernel,
        out_shape=(FIELD, FIELD) + (CELL,) * 6 + (Y_FACE, Y_FACE),
        in_specs=[VMEM] * 13,
        out_specs=(VMEM,) * 10,
        input_output_aliases={3 + i: i for i in range(10)},
        compiler_params=PARAMS,
        name="second",
    )(xb, xa, table, *state)
    state, (ya, yb) = out[:6], out[8:]
    yb = swapped(yb, "gy", 1)
    ya = swapped(ya, "gy", 0)
    state = pl.pallas_call(
        third_kernel,
        out_shape=(FIELD, FIELD) + (CELL,) * 4,
        in_specs=[VMEM] * 6,
        out_specs=(VMEM,) * 6,
        input_output_aliases={i: i for i in range(6)},
        compiler_params=PARAMS,
        cost_estimate=pl.CostEstimate(flops=20000000000, bytes_accessed=0, transcendentals=0),
        name="third",
    )(*state)
    state = pl.pallas_call(
        fourth_kernel,
        out_shape=(FIELD, FIELD) + (CELL,) * 4,
        in_specs=[VMEM] * 8,
        out_specs=(VMEM,) * 6,
        input_output_aliases={2 + i: i for i in range(6)},
        scratch_shapes=[pltpu.VMEM((XW, 8, LANES), F32), pltpu.VMEM((XW, 8, LANES), F32)],
        compiler_params=PARAMS,
        name="fourth",
    )(ya, table, *state)
    out = pl.pallas_call(
        last_kernel,
        out_shape=(
            jax.ShapeDtypeStruct(electric.shape, F32),
            jax.ShapeDtypeStruct(magnetic.shape, F32),
            FIELD,
            FIELD,
        )
        + (CELL,) * 4,
        in_specs=[VMEM] * 8,
        out_specs=(HBM, HBM) + (VMEM,) * 6,
        input_output_aliases={2 + i: 2 + i for i in range(6)},
        scratch_shapes=[
            pltpu.VMEM((XW, 8, LANES), F32),
            pltpu.VMEM((XW, 8, LANES), F32),
            pltpu.SemaphoreType.DMA((4, 6)),
        ],
        compiler_params=PARAMS,
        name="last",
    )(yb, table, *state)
    return out[0], out[1]


def solution(mesh):
    field = P(None, None, "gx", "gy", None)
    cell = P("gx", "gy", None)
    return jax.shard_map(
        per_device,
        mesh=mesh,
        in_specs=(field, field, cell, cell, P(), P(), P()),
        out_specs=(field, field),
        check_vma=False,
    )
```
